512 devices in a mesh: dp: 8 (over z_lo, x), dap: 64 (over z_hi, y, core).
Axes of the slice: x: 4, y: 8, z: 8 (z_hi: 4, z_lo: 2; z = z_hi * 2 + z_lo), core: 2. Of those that a mesh axis runs over, the one named last changes fastest.
Arguments:
- pair_act: bfloat16 [2048, 256, 128], P(('dp', 'dap')), parts along dimension 0, may hold values from -6 to 6
- cotangent: bfloat16 [2048, 256, 128], P(('dp', 'dap')), parts along dimension 0, may hold values from -16 to 16
- bias_start: bfloat16 [2048, 4, 256], P('dp'), parts along dimension 0, may hold values from -4 to 352
- bias_end: bfloat16 [2048, 4, 256], P('dp'), parts along dimension 0, may hold values from -4 to 352
- w_in_start: bfloat16 [128, 512], replicated, may hold values from -0.5 to 0.5
- w_out_start: bfloat16 [128, 128], replicated, may hold values from -0.5 to 0.5
- w_in_end: bfloat16 [128, 512], replicated, may hold values from -0.5 to 0.5
- w_out_end: bfloat16 [128, 128], replicated, may hold values from -0.5 to 0.5
- residue_mask: int32 [32768], P('dp'), parts along dimension 0, may hold values 0 or 1
- window_offset: int32 [8], P('dp'), parts along dimension 0, may hold values from 0 to 3840
Outputs:
- grad_pair: bfloat16 [2048, 256, 128], P(('dp', 'dap')), parts along dimension 0
- grad_bias_start: float32 [2048, 4, 256], P(('dp', 'dap')), parts along dimension 0
- grad_bias_end: float32 [2048, 4, 256], P(('dp', 'dap')), parts along dimension 0
- grad_in_start: float32 [1024, 512], P('dp'), parts along dimension 0
- grad_out_start: float32 [1024, 128], P('dp'), parts along dimension 0
- grad_in_end: float32 [1024, 512], P('dp'), parts along dimension 0
- grad_out_end: float32 [1024, 128], P('dp'), parts along dimension 0
The draws below stay inside these ranges and needn't reach their ends.
There are 8 independent parts, one for each index of `dp`. The reference program is written for one: setup_inputs(seed, part) draws one part's arguments, and reference() takes and returns one part's arrays. A program takes and returns all parts, laid end to end along the dimension named above; an argument that names none is the same for every part. Nothing has to cross between parts.
All inputs are finite; a program needn't handle non-finite values.
Results may differ from the reference program's by a relative error of at most 0.015.
Values may be sent and summed in bfloat16 or wider, within the bound.
No kernel may reach another device: no remote copies, remote signals or barrier semaphores. Data moves between devices by JAX's collectives and lax.ppermute only.
A program may use at most 64 MiB of HBM per device.

```python
import jax
import jax.numpy as jnp
from jax import lax

C = 128
H = 4
DH = 32
ROWS_DEV = 4
N = 256
CHAIN = 4096


def draw_bias_start(key, part):
    key = jax.random.fold_in(key, 11)
    base_key = jax.random.fold_in(key, 0)
    base_values = jnp.clip(jax.random.normal(base_key, (N, H, N), jnp.float32), -4.0, 4.0)
    return base_values.astype(jnp.bfloat16)


def draw_bias_end(key, part):
    key = jax.random.fold_in(key, 23)
    base_key = jax.random.fold_in(key, 0)
    base_values = jnp.clip(jax.random.normal(base_key, (N, H, N), jnp.float32), -4.0, 4.0)
    return base_values.astype(jnp.bfloat16)


def plant(result, own_key, low, top_value):
    longest = result.shape.index(max(result.shape))
    spots = []
    for shift in (0, 1):
        where = [jax.random.randint(jax.random.fold_in(own_key, axis), (), 0, length) for axis, length in enumerate(result.shape)]
        where[longest] = (where[longest] + shift) % result.shape[longest]
        spots.append(tuple(where))
    return result.at[spots[0]].set(low).at[spots[1]].set(top_value)


def with_spikes(array, rng, source, target, parts, factor):
    owner, partner = [(jnp.arange(array.shape[position]) // (array.shape[position] // parts)).reshape([-1 if axis == position else 1 for axis in range(array.ndim)]) for position in (source, target)]
    chosen = jax.random.permutation(rng, parts)[partner]
    strong = (owner == chosen) | (owner == (partner + parts // 2) % parts)
    return jnp.where(strong, factor * array, array)


def shard_levels(own_key, shape, shards, low, top_value):
    factor_of = 1.0
    for dim, blocks in shards:
        draws = jax.random.uniform(jax.random.fold_in(jax.random.fold_in(own_key, 6), dim), (blocks,), jnp.float32, low / len(shards), top_value / len(shards))
        factor_of = factor_of * jnp.repeat(jnp.exp(draws), shape[dim] // blocks).reshape((-1,) + (1,) * (len(shape) - 1 - dim))
    return factor_of


def scatter_about(own_key, shape, width, most, cuts=(), dtype=jnp.bfloat16):
    values = width * jax.random.normal(own_key, shape, jnp.float32)
    if cuts:
        values = values * shard_levels(own_key, shape, cuts, -0.22, 0.18)
    return jnp.clip(values, -most, most).astype(dtype)


def heavy_noise(stream_key, extent, width, reach, cuts, heavy, dtype=jnp.bfloat16):
    result = width * jax.random.normal(stream_key, extent, jnp.float32)
    if cuts:
        result = result * shard_levels(stream_key, extent, cuts, -0.22, 0.18)
    return jnp.clip(with_spikes(result, jax.random.fold_in(stream_key, 3), *heavy), -reach, reach).astype(dtype)


def setup_inputs(seed: int = 0, part: int = 0) -> dict:
    keys = jax.random.split(jax.random.key(seed), 11)
    own_keys = jax.random.split(jax.random.fold_in(keys[10], part), 11)
    pair_act = scatter_about(own_keys[0], (N, N, C), 1.0, 6.0, ((0, 64),))
    cotangent = heavy_noise(own_keys[1], (N, N, C), 1.0, 16.0, ((0, 64),), (0, 1, 64, 4.0))
    bias_start = draw_bias_start(jax.random.fold_in(jax.random.fold_in(keys[10], part), 71), part)
    bias_end = draw_bias_end(jax.random.fold_in(jax.random.fold_in(keys[10], part), 71), part)
    w_in_start = scatter_about(keys[4], (C, 4 * H * DH), C ** -0.5, 0.5)
    w_out_start = scatter_about(keys[5], (H * DH, C), (H * DH) ** -0.5, 0.5)
    w_in_end = scatter_about(keys[6], (C, 4 * H * DH), C ** -0.5, 0.5)
    w_out_end = scatter_about(keys[7], (H * DH, C), (H * DH) ** -0.5, 0.5)
    residue_mask = plant((jax.random.randint(own_keys[8], (CHAIN,), 0, 8) < 7).astype(jnp.int32), jax.random.fold_in(own_keys[8], 1), 0, 1)
    window_offset = jax.random.randint(own_keys[9], (1,), 0, CHAIN - N + 1).astype(jnp.int32)
    return {"pair_act": pair_act, "cotangent": cotangent, "bias_start": bias_start, "bias_end": bias_end, "w_in_start": w_in_start, "w_out_start": w_out_start, "w_in_end": w_in_end, "w_out_end": w_out_end, "residue_mask": residue_mask, "window_offset": window_offset}


ln_epsilon = 1e-05
mask_penalty = 1000000000.0

def product(formula, first_operand, second_operand):
    return jnp.einsum(formula, first_operand.astype(jnp.float32), second_operand.astype(jnp.float32))

def layer_stats(activations):
    values = activations.astype(jnp.float32)
    centred = values - lax.optimization_barrier(jnp.mean(values, axis=-1, keepdims=True))
    inv_std = lax.rsqrt(lax.optimization_barrier(jnp.mean(centred * centred, axis=-1, keepdims=True)) + ln_epsilon)
    return (centred * inv_std, inv_std)

def softmax_rows(queries, key_rows, pair_bias, penalty):
    scores = product('rjhd,rkhd->rjhk', queries, key_rows) + pair_bias.astype(jnp.float32)[None] + penalty
    row_peak = lax.optimization_barrier(jnp.max(scores, axis=-1, keepdims=True))
    exponent = jnp.exp(scores - row_peak)
    return exponent / lax.optimization_barrier(jnp.sum(exponent, axis=-1, keepdims=True))

def attention_forward(activations, pair_bias, penalty, w_in, w_out):
    row_count, length = (activations.shape[0], activations.shape[1])
    hidden = w_out.shape[0]
    normed_f32, inv_std = layer_stats(activations)
    normed = normed_f32.astype(jnp.bfloat16)
    projected = product('rjc,cf->rjf', normed, w_in)
    queries = (projected[..., :hidden] * DH ** (-0.5)).astype(jnp.bfloat16).reshape(row_count, length, H, DH)
    key_rows = projected[..., hidden:2 * hidden].astype(jnp.bfloat16).reshape(row_count, length, H, DH)
    value_rows = projected[..., 2 * hidden:3 * hidden].astype(jnp.bfloat16).reshape(row_count, length, H, DH)
    gate_value = jax.nn.sigmoid(projected[..., 3 * hidden:])
    probs_f32 = softmax_rows(queries, key_rows, pair_bias, penalty)
    probs_b16 = probs_f32.astype(jnp.bfloat16)
    attended = product('rjhk,rkhd->rjhd', probs_b16, value_rows).reshape(row_count, length, hidden)
    gated_out = (gate_value * attended).astype(jnp.bfloat16)
    output = (activations.astype(jnp.float32) + product('rjf,fc->rjc', gated_out, w_out)).astype(jnp.bfloat16)
    return (output, (normed_f32, inv_std, normed, queries, key_rows, value_rows, gate_value, attended, gated_out, probs_f32, probs_b16))

def attention_backward(state_tuple, upstream, w_in, w_out):
    normed_f32, inv_std, normed, queries, key_rows, value_rows, gate_value, attended, gated_out, probs_f32, probs_b16 = state_tuple
    row_count, length = (upstream.shape[0], upstream.shape[1])
    hidden = w_out.shape[0]
    grad_wout = product('rjf,rjc->fc', gated_out, upstream)
    grad_gated = product('rjc,fc->rjf', upstream, w_out)
    grad_gate = grad_gated * attended * gate_value * (1.0 - gate_value)
    grad_mixed = (grad_gated * gate_value).astype(jnp.bfloat16).reshape(row_count, length, H, DH)
    grad_probs = product('rjhd,rkhd->rjhk', grad_mixed, value_rows)
    grad_value = product('rjhk,rjhd->rkhd', probs_b16, grad_mixed)
    grad_scores = probs_f32 * (grad_probs - lax.optimization_barrier(jnp.sum(probs_f32 * grad_probs, axis=-1, keepdims=True)))
    scores_b16 = grad_scores.astype(jnp.bfloat16)
    grad_query = product('rjhk,rkhd->rjhd', scores_b16, key_rows) * DH ** (-0.5)
    grad_key = product('rjhk,rjhd->rkhd', scores_b16, queries)
    grad_proj = jnp.concatenate([grad_query.reshape(row_count, length, hidden), grad_key.reshape(row_count, length, hidden), grad_value.reshape(row_count, length, hidden), grad_gate], axis=-1).astype(jnp.bfloat16)
    grad_win = product('rjc,rjf->cf', normed, grad_proj)
    grad_normed = product('rjf,cf->rjc', grad_proj, w_in)
    centred_grad = grad_normed - lax.optimization_barrier(jnp.mean(grad_normed, axis=-1, keepdims=True)) - normed_f32 * lax.optimization_barrier(jnp.mean(grad_normed * normed_f32, axis=-1, keepdims=True))
    grad_block = upstream.astype(jnp.float32) + inv_std * centred_grad
    return (grad_block, grad_scores, grad_win, grad_wout, grad_mixed)

def reference(pair_act, cotangent, bias_start, bias_end, w_in_start, w_out_start, w_in_end, w_out_end, residue_mask, window_offset):
    window = lax.dynamic_slice_in_dim(residue_mask, window_offset[0], N)
    penalty = (window.astype(jnp.float32) - 1.0) * mask_penalty
    blocks = N // ROWS_DEV
    channels = pair_act.shape[2]

    def start_rows(activations):
        return attention_forward(activations, bias_start, penalty, w_in_start, w_out_start)[0]
    first_out = lax.map(start_rows, pair_act.reshape(blocks, ROWS_DEV, N, channels)).reshape(N, N, channels)

    def gradients(pair_bias, w_in, w_out):

        def one_block(operands):
            activations, upstream = operands
            state_tuple = attention_forward(activations, pair_bias, penalty, w_in, w_out)[1]
            grad_block, grad_scores, grad_win, grad_wout, unused = attention_backward(state_tuple, upstream, w_in, w_out)
            return (grad_block, lax.optimization_barrier(jnp.sum(grad_scores, axis=0)), grad_win, grad_wout)
        return one_block
    columns = jnp.swapaxes(first_out, 0, 1).reshape(blocks, ROWS_DEV, N, channels)
    upstream = jnp.swapaxes(cotangent, 0, 1).reshape(blocks, ROWS_DEV, N, channels)
    grad_cols, bias_end_terms, in_end_terms, out_end_terms = lax.map(gradients(bias_end, w_in_end, w_out_end), (columns, upstream))
    grad_first = jnp.swapaxes(grad_cols.reshape(N, N, channels), 0, 1).astype(jnp.bfloat16)
    grad_rows, bias_start_terms, in_start_terms, out_start_terms = lax.map(gradients(bias_start, w_in_start, w_out_start), (pair_act.reshape(blocks, ROWS_DEV, N, channels), grad_first.reshape(blocks, ROWS_DEV, N, channels)))
    return (grad_rows.reshape(N, N, channels).astype(jnp.bfloat16), lax.optimization_barrier(jnp.sum(bias_start_terms, axis=0)), lax.optimization_barrier(jnp.sum(bias_end_terms, axis=0)), lax.optimization_barrier(jnp.sum(in_start_terms, axis=0)) / N, lax.optimization_barrier(jnp.sum(out_start_terms, axis=0)) / N, lax.optimization_barrier(jnp.sum(in_end_terms, axis=0)) / N, lax.optimization_barrier(jnp.sum(out_end_terms, axis=0)) / N)
```

```python
import functools

import jax
import jax.numpy as jnp
from jax import lax
from jax.experimental import pallas as pl
from jax.experimental.pallas import tpu as pltpu
from jax.sharding import PartitionSpec as P

H = 4
DH = 32
N = 256
C = 128
R = 4
PEERS = N // R

LN_EPSILON = 1e-05
MASK_PENALTY = 1000000000.0

f32 = jnp.float32
bf16 = jnp.bfloat16

VMEM_LIMIT = 48 * 1024 * 1024


def dot(a, b, dims):
    return lax.dot_general(a, b, (dims, ((), ())), preferred_element_type=f32)


def nn(a, b):
    return dot(a, b, ((1,), (0,)))


def nt(a, b):
    return dot(a, b, ((1,), (1,)))


def head_masks():
    lane = lax.broadcasted_iota(jnp.int32, (N, C), 1) // DH
    return [lane == h for h in range(H)]


def masked(value, masks):
    zero = jnp.zeros_like(value)
    return [jnp.where(m, value, zero) for m in masks]


def layer_stats(values):
    centred = values - jnp.mean(values, axis=-1, keepdims=True)
    inv_std = lax.rsqrt(jnp.mean(centred * centred, axis=-1, keepdims=True) + LN_EPSILON)
    return centred * inv_std, inv_std


def project(normed, w_in):
    projected = nn(normed, w_in)
    queries = (projected[:, :C] * DH ** (-0.5)).astype(bf16)
    keys = projected[:, C : 2 * C].astype(bf16)
    values = projected[:, 2 * C : 3 * C].astype(bf16)
    gate = 1.0 / (1.0 + jnp.exp(-projected[:, 3 * C :]))
    return queries, keys, values, gate


def head_probs(key_h, queries, bias_h, penalty):
    scores = nt(key_h, queries) + bias_h.astype(f32) + penalty
    exponent = jnp.exp(scores - jnp.max(scores, axis=0, keepdims=True))
    return exponent * (1.0 / jnp.sum(exponent, axis=0, keepdims=True))


def pack_rows(value, r, stage, packed):
    stage[...] = value
    for residue in range(R):
        packed[pl.ds(r * R + residue, PEERS, stride=R * R), :] = stage[pl.ds(residue, PEERS, stride=R), :]


def start_forward_kernel(x_ref, cot_ref, bias_ref, pen_ref, w_in_ref, w_out_ref, send_ref, stage, first_packed, cot_packed):
    masks = head_masks()
    penalty = jnp.broadcast_to(pen_ref[...], (N, N))
    for r in range(R):
        x = x_ref[r].astype(f32)
        normed, _ = layer_stats(x)
        queries, keys, values, gate = project(normed.astype(bf16), w_in_ref[...])
        keys_h = masked(keys, masks)
        values_t = values.astype(f32).T.astype(bf16)
        attended_t = []
        for h in range(H):
            probs = head_probs(keys_h[h], queries, bias_ref[h], penalty)
            attended_t.append(nn(values_t[h * DH : (h + 1) * DH], probs.astype(bf16)))
        attended = jnp.concatenate(attended_t, axis=0).T
        gated = (gate * attended).astype(bf16)
        out = (x + nn(gated, w_out_ref[...])).astype(bf16).astype(f32)
        pack_rows(out, r, stage, first_packed)
        pack_rows(cot_ref[r].astype(f32), r, stage, cot_packed)
    send_ref[:, : R * R, :] = first_packed[...].reshape(PEERS, R * R, C).astype(bf16)
    send_ref[:, R * R :, :] = cot_packed[...].reshape(PEERS, R * R, C).astype(bf16)


def node_backward(
    r, x, upstream, bias_ref, penalty, w_in_ref, w_in_t_ref, w_out_ref, w_out_t_ref, masks, bias_sum, weight_sum
):
    normed, inv_std = layer_stats(x)
    normed_b = normed.astype(bf16)
    queries, keys, values, gate = project(normed_b, w_in_ref[...])
    keys_h = masked(keys, masks)
    values_h = masked(values, masks)
    values_t = values.astype(f32).T.astype(bf16)
    keys_t = keys.astype(f32).T.astype(bf16)
    probs = [head_probs(keys_h[h], queries, bias_ref[h], penalty) for h in range(H)]
    probs_b = [p.astype(bf16) for p in probs]
    attended = jnp.concatenate([nn(values_t[h * DH : (h + 1) * DH], probs_b[h]) for h in range(H)], axis=0).T
    gated = (gate * attended).astype(bf16)
    up_b = upstream.astype(bf16)
    grad_gated = nn(up_b, w_out_t_ref[...])
    grad_gate = grad_gated * attended * gate * (1.0 - gate)
    grad_mixed = (grad_gated * gate).astype(bf16)
    grad_value = jnp.zeros((N, C), f32)
    grad_key = jnp.zeros((N, C), f32)
    grad_query_t = []
    for h in range(H):
        grad_probs = nt(values_h[h], grad_mixed)
        inner = jnp.sum(probs[h] * grad_probs, axis=0, keepdims=True)
        grad_scores = probs[h] * (grad_probs - inner)
        if r == 0:
            bias_sum[h] = grad_scores
        else:
            bias_sum[h] += grad_scores
        scores_b = grad_scores.astype(bf16)
        grad_value = jnp.where(masks[h], nn(probs_b[h], grad_mixed), grad_value)
        grad_key = jnp.where(masks[h], nn(scores_b, queries), grad_key)
        grad_query_t.append(nn(keys_t[h * DH : (h + 1) * DH], scores_b))
    grad_query = jnp.concatenate(grad_query_t, axis=0).T * DH ** (-0.5)
    grad_proj = jnp.concatenate([grad_query, grad_key, grad_value, grad_gate], axis=-1).astype(bf16)
    win = nn(normed.T.astype(bf16), grad_proj)
    wout = nn(gated.astype(f32).T.astype(bf16), up_b)
    blocks = [win[:, q * C : (q + 1) * C] for q in range(4)] + [wout]
    for q, block in enumerate(blocks):
        if r == 0:
            weight_sum[q] = block
        else:
            weight_sum[q] += block
    grad_normed = nn(grad_proj, w_in_t_ref[...])
    centred = (
        grad_normed
        - jnp.mean(grad_normed, axis=-1, keepdims=True)
        - normed * jnp.mean(grad_normed * normed, axis=-1, keepdims=True)
    )
    return upstream + inv_std * centred


BIAS_ROWS = R * H * N // C
WEIGHT_ROWS = 16
WEIGHT_BLOCKS = 5


def pack_terms(bias_sum, weight_sum, bias_packed, weight_packed, bias_send, weight_send):
    eye = (lax.broadcasted_iota(jnp.int32, (N, N), 0) == lax.broadcasted_iota(jnp.int32, (N, N), 1)).astype(bf16)
    halves = N // C
    for h in range(H):
        by_query = nt(eye, bias_sum[h].astype(bf16))
        for half in range(halves):
            bias_packed[pl.ds(h * halves + half, N, stride=H * halves), :] = by_query[:, half * C : (half + 1) * C]
    bias_send[...] = bias_packed[...].reshape(PEERS, BIAS_ROWS, C).astype(bf16)
    weight_packed[...] = jnp.zeros_like(weight_packed)
    for q in range(WEIGHT_BLOCKS):
        for parity in range(2):
            block = weight_sum.at[q][pl.ds(parity, PEERS, stride=2), :]
            weight_packed[pl.ds(q * 2 + parity, PEERS, stride=WEIGHT_ROWS), :] = block
    weight_send[...] = weight_packed[...].reshape(PEERS, WEIGHT_ROWS, C).astype(bf16)


def end_kernel(
    recv_ref, bias_ref, pen_ref, w_in_ref, w_in_t_ref, w_out_ref, w_out_t_ref,
    send_ref, bias_send, weight_send,
    x_all, up_all, stage, grad_packed, bias_sum, weight_sum, bias_packed, weight_packed,
):
    masks = head_masks()
    penalty = jnp.broadcast_to(pen_ref[...], (N, N))
    x_all[...] = recv_ref[:, : R * R, :].astype(f32).reshape(N * R, C)
    up_all[...] = recv_ref[:, R * R :, :].astype(f32).reshape(N * R, C)
    for r in range(R):
        grad = node_backward(
            r, x_all[pl.ds(r, N, stride=R), :], up_all[pl.ds(r, N, stride=R), :],
            bias_ref, penalty, w_in_ref, w_in_t_ref, w_out_ref, w_out_t_ref, masks, bias_sum, weight_sum,
        )
        pack_rows(grad, r, stage, grad_packed)
    send_ref[...] = grad_packed[...].reshape(PEERS, R * R, C).astype(bf16)
    pack_terms(bias_sum, weight_sum, bias_packed, weight_packed, bias_send, weight_send)


def start_kernel(
    x_ref, recv_ref, bias_ref, pen_ref, w_in_ref, w_in_t_ref, w_out_ref, w_out_t_ref,
    grad_ref, bias_send, weight_send,
    up_all, bias_sum, weight_sum, bias_packed, weight_packed,
):
    masks = head_masks()
    penalty = jnp.broadcast_to(pen_ref[...], (N, N))
    up_all[...] = recv_ref[...].astype(f32).reshape(N * R, C)
    for r in range(R):
        grad = node_backward(
            r, x_ref[r].astype(f32), up_all[pl.ds(r, N, stride=R), :],
            bias_ref, penalty, w_in_ref, w_in_t_ref, w_out_ref, w_out_t_ref, masks, bias_sum, weight_sum,
        )
        grad_ref[r] = grad.astype(bf16)
    pack_terms(bias_sum, weight_sum, bias_packed, weight_packed, bias_send, weight_send)


def sum_kernel(recv_ref, out_ref):
    out_ref[...] = jnp.sum(recv_ref[...].astype(f32), axis=0)


def weight_sum_kernel(end_ref, start_ref, out_ref):
    for part, ref in enumerate((end_ref, start_ref)):
        total = jnp.sum(ref[...].astype(f32), axis=0).astype(bf16)
        out_ref[:, part * WEIGHT_ROWS : (part + 1) * WEIGHT_ROWS, :] = jnp.broadcast_to(
            total[None], (PEERS, WEIGHT_ROWS, C)
        )


def weight_unpack_kernel(recv_ref, in_start, out_start, in_end, out_end, stage, block):
    for part, (win, wout) in enumerate(((in_end, out_end), (in_start, out_start))):
        received = recv_ref[:, part * WEIGHT_ROWS : (part + 1) * WEIGHT_ROWS, :]
        stage[...] = received.astype(f32).reshape(PEERS * WEIGHT_ROWS, C) * (1.0 / N)
        for q in range(WEIGHT_BLOCKS):
            for parity in range(2):
                block[pl.ds(parity, PEERS, stride=2), :] = stage[pl.ds(q * 2 + parity, PEERS, stride=WEIGHT_ROWS), :]
            if q < 4:
                win[:, q * C : (q + 1) * C] = block[...]
            else:
                wout[...] = block[...]


def call(kernel, outs, scratch=()):
    vmem = pl.BlockSpec(memory_space=pltpu.VMEM)
    return pl.pallas_call(
        kernel,
        out_shape=outs,
        out_specs=jax.tree.map(lambda _: vmem, outs),
        scratch_shapes=list(scratch),
        compiler_params=pltpu.CompilerParams(vmem_limit_bytes=VMEM_LIMIT),
    )


def struct(shape, dtype):
    return jax.ShapeDtypeStruct(shape, dtype)


def exchange(value):
    return lax.all_to_all(value, "dap", split_axis=0, concat_axis=0, tiled=True)


TERM_SCRATCH = (
    pltpu.VMEM((H, N, N), f32),
    pltpu.VMEM((WEIGHT_BLOCKS, C, C), f32),
    pltpu.VMEM((N * H * N // C, C), f32),
    pltpu.VMEM((PEERS * WEIGHT_ROWS, C), f32),
)
TERM_OUTS = (struct((PEERS, BIAS_ROWS, C), bf16), struct((PEERS, WEIGHT_ROWS, C), bf16))


def shards(
    pair_act,
    cotangent,
    bias_start,
    bias_end,
    w_in_start,
    w_out_start,
    w_in_end,
    w_out_end,
    residue_mask,
    window_offset,
):
    window = lax.dynamic_slice_in_dim(residue_mask, window_offset[0], N)
    penalty = ((window.astype(f32) - 1.0) * MASK_PENALTY)[:, None]
    bias_start_t = jnp.transpose(bias_start, (1, 2, 0))
    bias_end_t = jnp.transpose(bias_end, (1, 2, 0))
    rows_f32 = pltpu.VMEM((N * R, C), f32)
    stage = pltpu.VMEM((N, C), f32)

    send = call(start_forward_kernel, struct((PEERS, 2 * R * R, C), bf16), (stage, rows_f32, rows_f32))(
        pair_act, cotangent, bias_start_t, penalty, w_in_start, w_out_start
    )
    recv = exchange(send)
    grad_send, bias_end_send, weight_end_send = call(
        end_kernel,
        (struct((PEERS, R * R, C), bf16),) + TERM_OUTS,
        (rows_f32, rows_f32, stage, rows_f32) + TERM_SCRATCH,
    )(recv, bias_end_t, penalty, w_in_end, w_in_end.T, w_out_end, w_out_end.T)
    grad_recv = exchange(grad_send)
    end_terms = exchange(jnp.concatenate([bias_end_send, weight_end_send], axis=1))
    grad_pair, bias_start_send, weight_start_send = call(
        start_kernel,
        (struct((R, N, C), bf16),) + TERM_OUTS,
        (rows_f32,) + TERM_SCRATCH,
    )(pair_act, grad_recv, bias_start_t, penalty, w_in_start, w_in_start.T, w_out_start, w_out_start.T)
    weight_start_recv = exchange(weight_start_send)
    bias_start_recv = exchange(bias_start_send)
    weight_send = call(weight_sum_kernel, struct((PEERS, 2 * WEIGHT_ROWS, C), bf16))(
        end_terms[:, BIAS_ROWS:], weight_start_recv
    )
    weight_recv = exchange(weight_send)
    grad_bias_end = call(sum_kernel, struct((BIAS_ROWS, C), f32))(end_terms[:, :BIAS_ROWS])
    grad_bias_start = call(sum_kernel, struct((BIAS_ROWS, C), f32))(bias_start_recv)
    weights = call(
        weight_unpack_kernel,
        tuple(struct(shape, f32) for shape in ((C, 4 * C), (C, C), (C, 4 * C), (C, C))),
        (pltpu.VMEM((PEERS * WEIGHT_ROWS, C), f32), pltpu.VMEM((C, C), f32)),
    )(weight_recv)
    return (
        grad_pair,
        grad_bias_start.reshape(R, H, N),
        grad_bias_end.reshape(R, H, N),
    ) + tuple(weights)


def solution(mesh):
    rows = P(("dp", "dap"), None, None)
    placed = (rows, rows, P("dp", None, None), P("dp", None, None), P(), P(), P(), P(), P("dp"), P("dp"))
    return jax.shard_map(
        shards,
        mesh=mesh,
        in_specs=placed,
        out_specs=(rows, rows, rows, P("dp", None), P("dp", None), P("dp", None), P("dp", None)),
        check_vma=False,
    )
```

```python
import functools

import jax
import jax.numpy as jnp
from jax import lax
from jax.experimental import pallas as pl
from jax.experimental.pallas import tpu as pltpu
from jax.sharding import PartitionSpec as P

H = 4
DH = 32
N = 256
C = 128
R = 4
PEERS = N // R

LN_EPSILON = 1e-05
MASK_PENALTY = 1000000000.0

f32 = jnp.float32
bf16 = jnp.bfloat16

VMEM_LIMIT = 40 * 1024 * 1024

GROUP = 4


def dot(a, b, dims):
    return lax.dot_general(a, b, (dims, ((), ())), preferred_element_type=f32)


def nn(a, b):
    return dot(a, b, ((1,), (0,)))


def nt(a, b):
    return dot(a, b, ((1,), (1,)))


def head_masks():
    lane = lax.broadcasted_iota(jnp.int32, (N, C), 1) // DH
    return [lane == h for h in range(H)]


def masked(value, masks):
    zero = jnp.zeros_like(value)
    return [jnp.where(m, value, zero) for m in masks]


def layer_stats(values):
    centred = values - jnp.mean(values, axis=-1, keepdims=True)
    inv_std = lax.rsqrt(jnp.mean(centred * centred, axis=-1, keepdims=True) + LN_EPSILON)
    return centred * inv_std, inv_std


def project(normed, w_in):
    projected = nn(normed, w_in)
    queries = (projected[:, :C] * DH ** (-0.5)).astype(bf16)
    keys = projected[:, C : 2 * C].astype(bf16)
    values = projected[:, 2 * C : 3 * C].astype(bf16)
    gate = 1.0 / (1.0 + jnp.exp(-projected[:, 3 * C :]))
    return queries, keys, values, gate


def pack_rows(value, r, stage, packed):
    stage[...] = value
    for residue in range(R):
        packed[pl.ds(r * R + residue, PEERS, stride=R * R), :] = stage[pl.ds(residue, PEERS, stride=R), :]


def softmax_all(keys_h, queries, bias_ref, penalty):
    scores = [[nt(keys_h[r][h], queries[r]) for h in range(H)] for r in range(len(queries))]
    return [[head_softmax(row[h], bias_ref[h], penalty) for h in range(H)] for row in scores]


def head_softmax(scores, bias_h, penalty):
    scores = scores + bias_h.astype(f32) + penalty
    exponent = jnp.exp(scores - jnp.max(scores, axis=0, keepdims=True))
    return exponent * (1.0 / jnp.sum(exponent, axis=0, keepdims=True))


def attend_all(values_t, probs_b):
    parts = [
        [nn(values_t[r][h * DH : (h + 1) * DH], probs_b[r][h]) for h in range(H)] for r in range(len(values_t))
    ]
    return [jnp.concatenate(row, axis=0).T for row in parts]


def start_forward_kernel(x_ref, cot_ref, bias_ref, pen_ref, w_in_ref, w_out_ref, send_ref, stage, first_packed, cot_packed):
    masks = head_masks()
    penalty = jnp.broadcast_to(pen_ref[...], (N, N))
    x = x_ref[...].reshape(R * N, C).astype(f32)
    normed, _ = layer_stats(x)
    queries, keys, values, gate = project(normed.astype(bf16), w_in_ref[...])
    attended = []
    for first in range(0, R, GROUP):
        rows = [slice(r * N, (r + 1) * N) for r in range(first, first + GROUP)]
        keys_h = [masked(keys[at], masks) for at in rows]
        values_t = [values[at].astype(f32).T.astype(bf16) for at in rows]
        probs = softmax_all(keys_h, [queries[at] for at in rows], bias_ref, penalty)
        attended += attend_all(values_t, [[p.astype(bf16) for p in row] for row in probs])
    gated = (gate * jnp.concatenate(attended, axis=0)).astype(bf16)
    out = (x + nn(gated, w_out_ref[...])).astype(bf16).astype(f32)
    for r in range(R):
        pack_rows(out[r * N : (r + 1) * N], r, stage.at[r], first_packed)
        pack_rows(cot_ref[r].astype(f32), r, stage.at[R + r], cot_packed)
    send_ref[:, : R * R, :] = first_packed[...].reshape(PEERS, R * R, C).astype(bf16)
    send_ref[:, R * R :, :] = cot_packed[...].reshape(PEERS, R * R, C).astype(bf16)


def node_states(x, bias_ref, penalty, w_in_ref, masks):
    count = x.shape[0] // N
    normed, inv_std = layer_stats(x)
    queries, keys, values, gate = project(normed.astype(bf16), w_in_ref[...])
    rows = [slice(r * N, (r + 1) * N) for r in range(count)]
    keys_h = [masked(keys[at], masks) for at in rows]
    values_t = [values[at].astype(f32).T.astype(bf16) for at in rows]
    keys_t = [keys[at].astype(f32).T.astype(bf16) for at in rows]
    probs = softmax_all(keys_h, [queries[at] for at in rows], bias_ref, penalty)
    attended = attend_all(values_t, [[p.astype(bf16) for p in row] for row in probs])
    return [
        (normed[at], inv_std[at], queries[at], keys_t[r], values[at], gate[at], attended[r], probs[r])
        for r, at in enumerate(rows)
    ]


def node_backward(first, states, upstreams, w_in_t_ref, w_out_t_ref, masks, bias_sum, weight_sum):
    count = len(states)
    normed, inv_std, queries, keys_t, values, gate, attended, probs = zip(*states)
    values_h = [masked(v, masks) for v in values]
    up_b = [u.astype(bf16) for u in upstreams]
    grad_gated = [nn(u, w_out_t_ref[...]) for u in up_b]
    gated = [(gate[r] * attended[r]).astype(bf16) for r in range(count)]
    grad_gate = [grad_gated[r] * attended[r] * gate[r] * (1.0 - gate[r]) for r in range(count)]
    grad_mixed = [(grad_gated[r] * gate[r]).astype(bf16) for r in range(count)]
    grad_probs = [[nt(values_h[r][h], grad_mixed[r]) for h in range(H)] for r in range(count)]
    scores_b = [[None] * H for _ in range(count)]
    for h in range(H):
        total = None
        for r in range(count):
            inner = jnp.sum(probs[r][h] * grad_probs[r][h], axis=0, keepdims=True)
            grad_scores = probs[r][h] * (grad_probs[r][h] - inner)
            scores_b[r][h] = grad_scores.astype(bf16)
            total = grad_scores if total is None else total + grad_scores
        if first:
            bias_sum[h] = total
        else:
            bias_sum[h] += total
    wins, wouts, grads = [], [], []
    by_value = [[nn(probs[r][h].astype(bf16), grad_mixed[r]) for h in range(H)] for r in range(count)]
    by_key = [[nn(scores_b[r][h], queries[r]) for h in range(H)] for r in range(count)]
    by_query = [[nn(keys_t[r][h * DH : (h + 1) * DH], scores_b[r][h]) for h in range(H)] for r in range(count)]
    for r in range(count):
        grad_value, grad_key = by_value[r][0], by_key[r][0]
        for h in range(1, H):
            grad_value = jnp.where(masks[h], by_value[r][h], grad_value)
            grad_key = jnp.where(masks[h], by_key[r][h], grad_key)
        grad_query = jnp.concatenate(by_query[r], axis=0).T * DH ** (-0.5)
        grad_proj = jnp.concatenate([grad_query, grad_key, grad_value, grad_gate[r]], axis=-1).astype(bf16)
        wins.append(nn(normed[r].T.astype(bf16), grad_proj))
        wouts.append(nn(gated[r].astype(f32).T.astype(bf16), up_b[r]))
        grad_normed = nn(grad_proj, w_in_t_ref[...])
        centred = (
            grad_normed
            - jnp.mean(grad_normed, axis=-1, keepdims=True)
            - normed[r] * jnp.mean(grad_normed * normed[r], axis=-1, keepdims=True)
        )
        grads.append(upstreams[r] + inv_std[r] * centred)
    win, wout = sum(wins[1:], wins[0]), sum(wouts[1:], wouts[0])
    blocks = [win[:, q * C : (q + 1) * C] for q in range(4)] + [wout]
    for q, block in enumerate(blocks):
        if first:
            weight_sum[q] = block
        else:
            weight_sum[q] += block
    return grads


CHUNKS = H * N // C
WEIGHT_BLOCKS = 5
BIAS_HALF = 2 * PEERS * CHUNKS
WEIGHT_HALF = WEIGHT_BLOCKS * PEERS
SEND_ROWS = 32
WEIGHT_ROWS = 16


def core_index():
    return lax.axis_index("dap") % 2


def row_parity():
    return (lax.axis_index("dap") // 2) % 2


def split_bias(bias_sum, bias_packed, core):
    eye = (lax.broadcasted_iota(jnp.int32, (N, N), 0) == lax.broadcasted_iota(jnp.int32, (N, N), 1)).astype(bf16)
    for h in range(H):
        by_query = nt(eye, bias_sum[h].astype(bf16))
        for half in range(N // C):
            bias_packed[pl.ds(half * H + h, N, stride=CHUNKS), :] = by_query[:, half * C : (half + 1) * C]
    terms = bias_packed[...].reshape(PEERS, R, CHUNKS, C)
    keep, give = [], []
    for parity in range(2):
        even, odd = terms[:, 2 * parity], terms[:, 2 * parity + 1]
        keep.append(jnp.where(core == 0, even, odd).reshape(PEERS * CHUNKS, C))
        give.append(jnp.where(core == 0, odd, even).reshape(PEERS * CHUNKS, C))
    return keep, give


def end_kernel(
    recv_ref, bias_ref, pen_ref, w_in_ref, w_in_t_ref, w_out_t_ref,
    send_ref, give_ref, keep_ref,
    x_all, up_all, stage, grad_packed, bias_sum, weight_sum, bias_packed,
):
    masks = head_masks()
    core = core_index()
    penalty = jnp.broadcast_to(pen_ref[...], (N, N))
    x_all[...] = recv_ref[:, : R * R, :].astype(f32).reshape(N * R, C)
    up_all[...] = recv_ref[:, R * R :, :].astype(f32).reshape(N * R, C)
    for first in range(0, R, GROUP):
        group = range(first, first + GROUP)
        x = jnp.concatenate([x_all[pl.ds(r, N, stride=R), :] for r in group], axis=0)
        states = node_states(x, bias_ref, penalty, w_in_ref, masks)
        upstreams = [up_all[pl.ds(r, N, stride=R), :] for r in group]
        grads = node_backward(first == 0, states, upstreams, w_in_t_ref, w_out_t_ref, masks, bias_sum, weight_sum)
        for r, grad in zip(group, grads):
            pack_rows(grad, r, stage.at[r], grad_packed)
    send_ref[...] = grad_packed[...].reshape(PEERS, R * R, C).astype(bf16)
    keep, give = split_bias(bias_sum, bias_packed, core)
    for parity in range(2):
        rows = pl.ds(parity * PEERS * CHUNKS, PEERS * CHUNKS)
        keep_ref[rows, :] = keep[parity]
        give_ref[rows, :] = give[parity].astype(bf16)
    for q in range(WEIGHT_BLOCKS):
        even = weight_sum.at[q][pl.ds(0, PEERS, stride=2), :]
        odd = weight_sum.at[q][pl.ds(1, PEERS, stride=2), :]
        rows = pl.ds(BIAS_HALF + q * PEERS, PEERS)
        keep_ref[rows, :] = jnp.where(core == 0, even, odd)
        give_ref[rows, :] = jnp.where(core == 0, odd, even).astype(bf16)


def start_kernel(
    x_ref, recv_ref, bias_ref, pen_ref, w_in_ref, w_in_t_ref, w_out_t_ref, end_keep_ref, end_got_ref,
    grad_ref, send_ref, give_ref, keep_ref,
    up_all, bias_sum, weight_sum, bias_packed, weight_packed,
):
    masks = head_masks()
    core = core_index()
    penalty = jnp.broadcast_to(pen_ref[...], (N, N))
    up_all[...] = recv_ref[...].astype(f32).reshape(N * R, C)
    for first in range(0, R, GROUP):
        group = range(first, first + GROUP)
        x = x_ref[first : first + GROUP].reshape(GROUP * N, C).astype(f32)
        states = node_states(x, bias_ref, penalty, w_in_ref, masks)
        upstreams = [up_all[pl.ds(r, N, stride=R), :] for r in group]
        grads = node_backward(first == 0, states, upstreams, w_in_t_ref, w_out_t_ref, masks, bias_sum, weight_sum)
        for r, grad in zip(group, grads):
            grad_ref[r] = grad.astype(bf16)
    end_terms = end_keep_ref[...] + end_got_ref[...].astype(f32)
    weight_packed[...] = jnp.zeros_like(weight_packed)
    for q in range(WEIGHT_BLOCKS):
        for parity in range(2):
            block = weight_sum.at[q][pl.ds(parity, PEERS, stride=2), :]
            weight_packed[pl.ds(q * 2 + parity, PEERS, stride=WEIGHT_ROWS), :] = block
        block = end_terms[BIAS_HALF + q * PEERS : BIAS_HALF + (q + 1) * PEERS]
        weight_packed[pl.ds(2 * WEIGHT_BLOCKS + q, PEERS, stride=WEIGHT_ROWS), :] = block
    end_bias = [
        end_terms[parity * PEERS * CHUNKS : (parity + 1) * PEERS * CHUNKS].reshape(PEERS, CHUNKS, C)
        for parity in range(2)
    ]
    weights = weight_packed[...].reshape(PEERS, WEIGHT_ROWS, C)
    send_ref[...] = jnp.concatenate(end_bias + [weights], axis=1).astype(bf16)
    keep, give = split_bias(bias_sum, bias_packed, core)
    for parity in range(2):
        rows = pl.ds(parity * PEERS * CHUNKS, PEERS * CHUNKS)
        keep_ref[rows, :] = keep[parity]
        give_ref[rows, :] = give[parity].astype(bf16)


def pair_sum_kernel(keep_ref, got_ref, next_keep_ref, next_give_ref):
    total = keep_ref[...] + got_ref[...].astype(f32)
    low, high = total[: PEERS * CHUNKS], total[PEERS * CHUNKS :]
    parity = row_parity()
    next_keep_ref[...] = jnp.where(parity == 0, low, high)
    next_give_ref[...] = jnp.where(parity == 0, high, low).astype(bf16)


def write_bias(rows, out_ref):
    for residue in range(R):
        for half in range(N // C):
            out_ref[residue, :, half * C : (half + 1) * C] = rows[residue][half * H : (half + 1) * H]


def middle_kernel(recv_ref, keep_ref, got_ref, bias_ref, send_ref):
    by_core = jnp.sum(recv_ref[...].astype(f32).reshape(PEERS // 2, 2, SEND_ROWS, C), axis=0)
    end_bias = [by_core[core, parity * CHUNKS : (parity + 1) * CHUNKS] for parity in range(2) for core in range(2)]
    write_bias(end_bias, bias_ref)
    even, odd = by_core[0, 2 * CHUNKS :], by_core[1, 2 * CHUNKS :]
    slot = lax.broadcasted_iota(jnp.int32, (WEIGHT_ROWS, C), 0)
    totals = jnp.concatenate([even + jnp.where(slot < 2 * WEIGHT_BLOCKS, odd, 0.0), odd[CHUNKS:]], axis=0)
    bias_terms = (keep_ref[...] + got_ref[...].astype(f32)).reshape(PEERS, CHUNKS, C)
    everyone = jnp.broadcast_to(totals[None], (PEERS, SEND_ROWS - CHUNKS, C))
    send_ref[...] = jnp.concatenate([bias_terms, everyone], axis=1).astype(bf16)


def last_kernel(recv_ref, bias_ref, in_start, out_start, in_end, out_end, stage, block):
    received = recv_ref[...].astype(f32)
    write_bias(jnp.sum(received[:, :CHUNKS].reshape(PEERS // R, R, CHUNKS, C), axis=0), bias_ref)
    span = SEND_ROWS - CHUNKS
    stage[...] = received[:, CHUNKS:].reshape(PEERS * span, C) * (1.0 / N)
    end_slots = (2 * WEIGHT_BLOCKS, WEIGHT_ROWS + 2 * WEIGHT_BLOCKS - CHUNKS)
    for part, (win, wout) in enumerate(((in_start, out_start), (in_end, out_end))):
        for q in range(WEIGHT_BLOCKS):
            for parity in range(2):
                row = q * 2 + parity if part == 0 else end_slots[parity] + q
                block[pl.ds(parity, PEERS, stride=2), :] = stage[pl.ds(row, PEERS, stride=span), :]
            if q < 4:
                win[:, q * C : (q + 1) * C] = block[...]
            else:
                wout[...] = block[...]


def call(kernel, outs, scratch=(), far=()):
    vmem = pl.BlockSpec(memory_space=pltpu.VMEM)

    def apply(*operands):
        placed = [pltpu.with_memory_space_constraint(v, pltpu.HBM) if i in far else v for i, v in enumerate(operands)]
        return pl.pallas_call(
            kernel,
            out_shape=outs,
            in_specs=[vmem] * len(operands),
            out_specs=jax.tree.map(lambda _: vmem, outs),
            scratch_shapes=list(scratch),
            compiler_params=pltpu.CompilerParams(vmem_limit_bytes=VMEM_LIMIT),
        )(*placed)

    return apply


def struct(shape, dtype):
    return jax.ShapeDtypeStruct(shape, dtype)


def exchange(value):
    return lax.all_to_all(value, "dap", split_axis=0, concat_axis=0, tiled=True)


def swap(value, distance):
    return lax.ppermute(value, "dap", [(i, i ^ distance) for i in range(PEERS)])


def shards(
    pair_act,
    cotangent,
    bias_start,
    bias_end,
    w_in_start,
    w_out_start,
    w_in_end,
    w_out_end,
    residue_mask,
    window_offset,
):
    window = lax.dynamic_slice_in_dim(residue_mask, window_offset[0], N)
    penalty = ((window.astype(f32) - 1.0) * MASK_PENALTY)[:, None]
    bias_start_t = jnp.transpose(bias_start, (1, 2, 0))
    bias_end_t = jnp.transpose(bias_end, (1, 2, 0))
    rows_f32 = pltpu.VMEM((N * R, C), f32)
    bias_sum = pltpu.VMEM((H, N, N), f32)
    weight_sum = pltpu.VMEM((WEIGHT_BLOCKS, C, C), f32)
    bias_packed = pltpu.VMEM((N * CHUNKS, C), f32)
    weight_packed = pltpu.VMEM((PEERS * WEIGHT_ROWS, C), f32)
    term_rows = PEERS * CHUNKS

    send = call(start_forward_kernel, struct((PEERS, 2 * R * R, C), bf16), (pltpu.VMEM((2 * R, N, C), f32), rows_f32, rows_f32))(
        pair_act, cotangent, bias_start_t, penalty, w_in_start, w_out_start
    )
    recv = exchange(send)
    grad_send, end_give, end_keep = call(
        end_kernel,
        (
            struct((PEERS, R * R, C), bf16),
            struct((BIAS_HALF + WEIGHT_HALF, C), bf16),
            struct((BIAS_HALF + WEIGHT_HALF, C), f32),
        ),
        (rows_f32, rows_f32, pltpu.VMEM((R, N, C), f32), rows_f32, bias_sum, weight_sum, bias_packed),
    )(recv, bias_end_t, penalty, w_in_end, w_in_end.T, w_out_end.T)
    grad_recv = exchange(grad_send)
    end_got = swap(end_give, 1)
    grad_pair, term_send, start_give, start_keep = call(
        start_kernel,
        (
            struct((R, N, C), bf16),
            struct((PEERS, SEND_ROWS, C), bf16),
            struct((BIAS_HALF, C), bf16),
            struct((BIAS_HALF, C), f32),
        ),
        (rows_f32, bias_sum, weight_sum, bias_packed, weight_packed),
    )(pair_act, grad_recv, bias_start_t, penalty, w_in_start, w_in_start.T, w_out_start.T, end_keep, end_got)
    term_recv = exchange(term_send)
    pair_keep, pair_give = call(pair_sum_kernel, (struct((term_rows, C), f32), struct((term_rows, C), bf16)))(
        start_keep, swap(start_give, 1)
    )
    pair_got = swap(pair_give, 2)
    grad_bias_end, last_send = call(
        middle_kernel, (struct((R, H, N), f32), struct((PEERS, SEND_ROWS, C), bf16))
    )(term_recv, pair_keep, pair_got)
    last_recv = exchange(last_send)
    grad_bias_start, *weights = call(
        last_kernel,
        (struct((R, H, N), f32),) + tuple(struct(shape, f32) for shape in ((C, 4 * C), (C, C), (C, 4 * C), (C, C))),
        (pltpu.VMEM((PEERS * (SEND_ROWS - CHUNKS), C), f32), pltpu.VMEM((C, C), f32)),
    )(last_recv)
    return (grad_pair, grad_bias_start, grad_bias_end, *weights)


def solution(mesh):
    rows = P(("dp", "dap"), None, None)
    placed = (rows, rows, P("dp", None, None), P("dp", None, None), P(), P(), P(), P(), P("dp"), P("dp"))
    return jax.shard_map(
        shards,
        mesh=mesh,
        in_specs=placed,
        out_specs=(rows, rows, rows, P("dp", None), P("dp", None), P("dp", None), P("dp", None)),
        check_vma=False,
    )
```

```python
import functools

import jax
import jax.numpy as jnp
from jax import lax
from jax.experimental import pallas as pl
from jax.experimental.pallas import tpu as pltpu
from jax.sharding import PartitionSpec as P

H = 4
DH = 32
N = 256
C = 128
CHAIN = 4096
R = 4
PEERS = N // R

LN_EPSILON = 1e-05
MASK_PENALTY = 1000000000.0

f32 = jnp.float32
bf16 = jnp.bfloat16

VMEM_LIMIT = 20 * 1024 * 1024

GROUP = 4


def dot(a, b, dims):
    return lax.dot_general(a, b, (dims, ((), ())), preferred_element_type=f32)


def nn(a, b):
    return dot(a, b, ((1,), (0,)))


def nt(a, b):
    return dot(a, b, ((1,), (1,)))


def head_masks():
    lane = lax.broadcasted_iota(jnp.int32, (N, C), 1) // DH
    return [lane == h for h in range(H)]


def masked(value, masks):
    zero = jnp.zeros_like(value)
    return [jnp.where(m, value, zero) for m in masks]


def layer_stats(values):
    centred = values - jnp.mean(values, axis=-1, keepdims=True)
    inv_std = lax.rsqrt(jnp.mean(centred * centred, axis=-1, keepdims=True) + LN_EPSILON)
    return centred * inv_std, inv_std


def project(normed, w_in):
    projected = nn(normed, w_in)
    queries = (projected[:, :C] * DH ** (-0.5)).astype(bf16)
    keys = projected[:, C : 2 * C].astype(bf16)
    values = projected[:, 2 * C : 3 * C].astype(bf16)
    gate = 1.0 / (1.0 + jnp.exp(-projected[:, 3 * C :]))
    return queries, keys, values, gate


def pack_rows(value, r, stage, packed):
    stage[...] = value
    for residue in range(R):
        packed[pl.ds(r * R + residue, PEERS, stride=R * R), :] = stage[pl.ds(residue, PEERS, stride=R), :]


def softmax_all(keys_h, queries, bias_ref, penalty):
    scores = [[nt(keys_h[r][h], queries[r]) for h in range(H)] for r in range(len(queries))]
    return [[head_softmax(row[h], bias_ref[h], penalty) for h in range(H)] for row in scores]


def head_softmax(scores, bias_h, penalty):
    scores = scores + bias_h.astype(f32) + penalty
    exponent = jnp.exp(scores - jnp.max(scores, axis=0, keepdims=True))
    return exponent * (1.0 / jnp.sum(exponent, axis=0, keepdims=True))


def attend_all(values_t, probs_b):
    parts = [
        [nn(values_t[r][h * DH : (h + 1) * DH], probs_b[r][h]) for h in range(H)] for r in range(len(values_t))
    ]
    return [jnp.concatenate(row, axis=0).T for row in parts]


def window_penalty(mask_ref, offset_ref):
    rows = CHAIN // C
    offset = offset_ref[0]
    first, shift = offset // C, offset % C
    back = jnp.where(shift == 0, 0, C - shift)
    lane = lax.broadcasted_iota(jnp.int32, (8, C), 1)
    turned = []
    for i in range(N // C + 1):
        row = jnp.broadcast_to(mask_ref[pl.ds(jnp.minimum(first + i, rows - 1), 1), :], (8, C))
        turned.append(pltpu.roll(row, back, 1))
    columns = []
    for i in range(N // C):
        window = jnp.where(lane + shift < C, turned[i], turned[i + 1])
        penalty = (window.astype(f32) - 1.0) * MASK_PENALTY
        columns.append(jnp.broadcast_to(penalty[:1], (C, C)).T)
    return jnp.concatenate(columns, axis=0)


def wide_penalty(penalty):
    return jnp.concatenate([penalty] * (N // C), axis=1)


def start_forward_kernel(
    x_ref, cot_ref, bias_ref, mask_ref, offset_ref, w_in_ref, w_out_ref,
    send_ref, pen_ref, stage, first_packed, cot_packed,
):
    masks = head_masks()
    column = window_penalty(mask_ref, offset_ref)
    pen_ref[...] = column
    penalty = wide_penalty(column)
    x = x_ref[...].reshape(R * N, C).astype(f32)
    normed, _ = layer_stats(x)
    queries, keys, values, gate = project(normed.astype(bf16), w_in_ref[...])
    attended = []
    for first in range(0, R, GROUP):
        rows = [slice(r * N, (r + 1) * N) for r in range(first, first + GROUP)]
        keys_h = [masked(keys[at], masks) for at in rows]
        values_t = [values[at].astype(f32).T.astype(bf16) for at in rows]
        probs = softmax_all(keys_h, [queries[at] for at in rows], bias_ref, penalty)
        attended += attend_all(values_t, [[p.astype(bf16) for p in row] for row in probs])
    gated = (gate * jnp.concatenate(attended, axis=0)).astype(bf16)
    out = (x + nn(gated, w_out_ref[...])).astype(bf16).astype(f32)
    for r in range(R):
        pack_rows(out[r * N : (r + 1) * N], r, stage.at[r], first_packed)
        pack_rows(cot_ref[r].astype(f32), r, stage.at[R + r], cot_packed)
    send_ref[:, : R * R, :] = first_packed[...].reshape(PEERS, R * R, C).astype(bf16)
    send_ref[:, R * R :, :] = cot_packed[...].reshape(PEERS, R * R, C).astype(bf16)


def node_states(x, bias_ref, penalty, w_in_ref, masks):
    count = x.shape[0] // N
    normed, inv_std = layer_stats(x)
    queries, keys, values, gate = project(normed.astype(bf16), w_in_ref[...])
    rows = [slice(r * N, (r + 1) * N) for r in range(count)]
    keys_h = [masked(keys[at], masks) for at in rows]
    values_t = [values[at].astype(f32).T.astype(bf16) for at in rows]
    keys_t = [keys[at].astype(f32).T.astype(bf16) for at in rows]
    probs = softmax_all(keys_h, [queries[at] for at in rows], bias_ref, penalty)
    attended = attend_all(values_t, [[p.astype(bf16) for p in row] for row in probs])
    return [
        (normed[at], inv_std[at], queries[at], keys_t[r], values[at], gate[at], attended[r], probs[r])
        for r, at in enumerate(rows)
    ]


def node_backward(first, states, upstreams, w_in_t_ref, w_out_t_ref, masks, bias_sum, weight_sum):
    count = len(states)
    normed, inv_std, queries, keys_t, values, gate, attended, probs = zip(*states)
    values_h = [masked(v, masks) for v in values]
    up_b = [u.astype(bf16) for u in upstreams]
    grad_gated = [nn(u, w_out_t_ref[...]) for u in up_b]
    gated = [(gate[r] * attended[r]).astype(bf16) for r in range(count)]
    grad_gate = [grad_gated[r] * attended[r] * gate[r] * (1.0 - gate[r]) for r in range(count)]
    grad_mixed = [(grad_gated[r] * gate[r]).astype(bf16) for r in range(count)]
    grad_probs = [[nt(values_h[r][h], grad_mixed[r]) for h in range(H)] for r in range(count)]
    scores_b = [[None] * H for _ in range(count)]
    for h in range(H):
        total = None
        for r in range(count):
            inner = jnp.sum(probs[r][h] * grad_probs[r][h], axis=0, keepdims=True)
            grad_scores = probs[r][h] * (grad_probs[r][h] - inner)
            scores_b[r][h] = grad_scores.astype(bf16)
            total = grad_scores if total is None else total + grad_scores
        if first:
            bias_sum[h] = total
        else:
            bias_sum[h] += total
    wins, wouts, grads = [], [], []
    by_value = [[nn(probs[r][h].astype(bf16), grad_mixed[r]) for h in range(H)] for r in range(count)]
    by_key = [[nn(scores_b[r][h], queries[r]) for h in range(H)] for r in range(count)]
    by_query = [[nn(keys_t[r][h * DH : (h + 1) * DH], scores_b[r][h]) for h in range(H)] for r in range(count)]
    for r in range(count):
        grad_value, grad_key = by_value[r][0], by_key[r][0]
        for h in range(1, H):
            grad_value = jnp.where(masks[h], by_value[r][h], grad_value)
            grad_key = jnp.where(masks[h], by_key[r][h], grad_key)
        grad_query = jnp.concatenate(by_query[r], axis=0).T * DH ** (-0.5)
        grad_proj = jnp.concatenate([grad_query, grad_key, grad_value, grad_gate[r]], axis=-1).astype(bf16)
        wins.append(nn(normed[r].T.astype(bf16), grad_proj))
        wouts.append(nn(gated[r].astype(f32).T.astype(bf16), up_b[r]))
        grad_normed = nn(grad_proj, w_in_t_ref[...])
        centred = (
            grad_normed
            - jnp.mean(grad_normed, axis=-1, keepdims=True)
            - normed[r] * jnp.mean(grad_normed * normed[r], axis=-1, keepdims=True)
        )
        grads.append(upstreams[r] + inv_std[r] * centred)
    win, wout = sum(wins[1:], wins[0]), sum(wouts[1:], wouts[0])
    blocks = [win[:, q * C : (q + 1) * C] for q in range(4)] + [wout]
    for q, block in enumerate(blocks):
        if first:
            weight_sum[q] = block
        else:
            weight_sum[q] += block
    return grads


CHUNKS = H * N // C
WEIGHT_BLOCKS = 5
BIAS_HALF = 2 * PEERS * CHUNKS
WEIGHT_HALF = WEIGHT_BLOCKS * PEERS
WEIGHT_ROWS = 16
TERM_ROWS = 2 * CHUNKS + WEIGHT_ROWS
TOTAL_ROWS = WEIGHT_ROWS + CHUNKS


CHIPS = PEERS // 2


def core_index():
    return lax.axis_index("core")


def bias_terms(bias_sum, bias_packed):
    eye = (lax.broadcasted_iota(jnp.int32, (N, N), 0) == lax.broadcasted_iota(jnp.int32, (N, N), 1)).astype(bf16)
    for h in range(H):
        by_query = nt(eye, bias_sum[h].astype(bf16))
        for half in range(N // C):
            bias_packed[pl.ds(half * H + h, N, stride=CHUNKS), :] = by_query[:, half * C : (half + 1) * C]
    return bias_packed[...].reshape(PEERS, R, CHUNKS, C)


def core_split(even, odd, core, keep_ref, give_ref, rows):
    keep_ref[rows, :] = jnp.where(core == 0, even, odd)
    give_ref[rows, :] = jnp.where(core == 0, odd, even).astype(bf16)


def end_kernel(
    recv_ref, bias_ref, pen_ref, w_in_ref, w_in_t_ref, w_out_t_ref,
    send_ref, give_ref, keep_ref,
    x_all, up_all, stage, grad_packed, bias_sum, weight_sum, bias_packed,
):
    masks = head_masks()
    core = core_index()
    penalty = wide_penalty(pen_ref[...])
    x_all[...] = recv_ref[:, : R * R, :].astype(f32).reshape(N * R, C)
    up_all[...] = recv_ref[:, R * R :, :].astype(f32).reshape(N * R, C)
    for first in range(0, R, GROUP):
        group = range(first, first + GROUP)
        x = jnp.concatenate([x_all[pl.ds(r, N, stride=R), :] for r in group], axis=0)
        states = node_states(x, bias_ref, penalty, w_in_ref, masks)
        upstreams = [up_all[pl.ds(r, N, stride=R), :] for r in group]
        grads = node_backward(first == 0, states, upstreams, w_in_t_ref, w_out_t_ref, masks, bias_sum, weight_sum)
        for r, grad in zip(group, grads):
            pack_rows(grad, r, stage.at[r], grad_packed)
    send_ref[...] = grad_packed[...].reshape(PEERS, R * R, C).astype(bf16)
    terms = bias_terms(bias_sum, bias_packed)
    for parity in range(2):
        even, odd = (terms[:, 2 * parity + i].reshape(PEERS * CHUNKS, C) for i in range(2))
        core_split(even, odd, core, keep_ref, give_ref, pl.ds(parity * PEERS * CHUNKS, PEERS * CHUNKS))
    for q in range(WEIGHT_BLOCKS):
        even, odd = (weight_sum.at[q][pl.ds(i, PEERS, stride=2), :] for i in range(2))
        core_split(even, odd, core, keep_ref, give_ref, pl.ds(BIAS_HALF + q * PEERS, PEERS))


def start_kernel(
    x_ref, recv_ref, bias_ref, pen_ref, w_in_ref, w_in_t_ref, w_out_t_ref, end_keep_ref, end_got_ref,
    grad_ref, send_ref, give_ref, keep_ref,
    up_all, bias_sum, weight_sum, bias_packed, weight_packed,
):
    masks = head_masks()
    core = core_index()
    penalty = wide_penalty(pen_ref[...])
    up_all[...] = recv_ref[...].astype(f32).reshape(N * R, C)
    for first in range(0, R, GROUP):
        group = range(first, first + GROUP)
        x = x_ref[first : first + GROUP].reshape(GROUP * N, C).astype(f32)
        states = node_states(x, bias_ref, penalty, w_in_ref, masks)
        upstreams = [up_all[pl.ds(r, N, stride=R), :] for r in group]
        grads = node_backward(first == 0, states, upstreams, w_in_t_ref, w_out_t_ref, masks, bias_sum, weight_sum)
        for r, grad in zip(group, grads):
            grad_ref[r] = grad.astype(bf16)
    end_terms = end_keep_ref[...] + end_got_ref[...].astype(f32)
    weight_packed[...] = jnp.zeros_like(weight_packed)
    for q in range(WEIGHT_BLOCKS):
        for parity in range(2):
            block = weight_sum.at[q][pl.ds(parity, PEERS, stride=2), :]
            weight_packed[pl.ds(q * 2 + parity, PEERS, stride=WEIGHT_ROWS), :] = block
        block = end_terms[BIAS_HALF + q * PEERS : BIAS_HALF + (q + 1) * PEERS]
        weight_packed[pl.ds(2 * WEIGHT_BLOCKS + q, PEERS, stride=WEIGHT_ROWS), :] = block
    end_bias = by_parity(end_terms[:BIAS_HALF])
    weights = weight_packed[...].reshape(PEERS, WEIGHT_ROWS, C)
    send_ref[...] = jnp.concatenate(end_bias + [weights], axis=1).astype(bf16)
    terms = bias_terms(bias_sum, bias_packed).reshape(CHIPS, 2, R * CHUNKS, C)
    even, odd = (terms[:, i].reshape(BIAS_HALF, C) for i in range(2))
    core_split(even, odd, core, keep_ref, give_ref, slice(None))


def by_parity(rows):
    return [
        rows[parity * PEERS * CHUNKS : (parity + 1) * PEERS * CHUNKS].reshape(PEERS, CHUNKS, C) for parity in range(2)
    ]


def write_bias(rows, residue, out_ref):
    for half in range(N // C):
        out_ref[residue, :, half * C : (half + 1) * C] = rows[half * H : (half + 1) * H]


def middle_kernel(recv_ref, keep_ref, got_ref, send_ref, bias_ref):
    by_core = jnp.sum(recv_ref[...].astype(f32).reshape(CHIPS, 2, TERM_ROWS, C), axis=0)
    for parity in range(2):
        for core in range(2):
            write_bias(by_core[core, parity * CHUNKS : (parity + 1) * CHUNKS], 2 * parity + core, bias_ref)
    even, odd = by_core[0, 2 * CHUNKS :], by_core[1, 2 * CHUNKS :]
    slot = lax.broadcasted_iota(jnp.int32, (WEIGHT_ROWS, C), 0)
    totals = jnp.concatenate([even + jnp.where(slot < 2 * WEIGHT_BLOCKS, odd, 0.0), odd[CHUNKS:]], axis=0)
    bias_rows = (keep_ref[...] + got_ref[...].astype(f32)).reshape(CHIPS, R * CHUNKS, C)
    everyone = jnp.broadcast_to(totals[None], (CHIPS, TOTAL_ROWS, C))
    send_ref[...] = jnp.concatenate([bias_rows, everyone], axis=1).astype(bf16)


def totals_kernel(recv_ref, totals_ref):
    totals_ref[...] = recv_ref[...].astype(f32)[:, R * CHUNKS :].astype(bf16)


def last_kernel(recv_ref, totals_ref, bias_ref, in_start, out_start, in_end, out_end, stage, block):
    bias = jnp.sum(recv_ref[...].astype(f32)[:, : R * CHUNKS], axis=0)
    for residue in range(R):
        write_bias(bias[residue * CHUNKS : (residue + 1) * CHUNKS], residue, bias_ref)
    stage[...] = totals_ref[...].astype(f32).reshape(PEERS * TOTAL_ROWS, C) * (1.0 / N)
    end_slots = (2 * WEIGHT_BLOCKS, WEIGHT_ROWS + 2 * WEIGHT_BLOCKS - CHUNKS)
    for part, (win, wout) in enumerate(((in_start, out_start), (in_end, out_end))):
        for q in range(WEIGHT_BLOCKS):
            for core in range(2):
                for parity in range(2):
                    row = q * 2 + parity if part == 0 else end_slots[parity] + q
                    value = stage[pl.ds(core * CHIPS * TOTAL_ROWS + row, CHIPS, stride=TOTAL_ROWS), :]
                    block[pl.ds(2 * core + parity, CHIPS, stride=4), :] = value
            if q < 4:
                win[:, q * C : (q + 1) * C] = block[...]
            else:
                wout[...] = block[...]


def call(kernel, outs, scratch=(), places=None):
    vmem = pl.BlockSpec(memory_space=pltpu.VMEM)
    places = places or {}

    def apply(*operands):
        return pl.pallas_call(
            kernel,
            out_shape=outs,
            in_specs=[pl.BlockSpec(memory_space=places[i]) if i in places else vmem for i in range(len(operands))],
            out_specs=jax.tree.map(lambda _: vmem, outs),
            scratch_shapes=list(scratch),
            compiler_params=pltpu.CompilerParams(vmem_limit_bytes=VMEM_LIMIT),
        )(*operands)

    return apply


def struct(shape, dtype):
    return jax.ShapeDtypeStruct(shape, dtype)


def exchange(value, axes=("chip", "core")):
    rows = value.reshape(-1, C)
    return lax.all_to_all(rows, axes, split_axis=0, concat_axis=0, tiled=True).reshape(value.shape)


def swap(value):
    return lax.ppermute(value, "core", [(0, 1), (1, 0)])


def shards(
    pair_act,
    cotangent,
    bias_start,
    bias_end,
    w_in_start,
    w_out_start,
    w_in_end,
    w_out_end,
    residue_mask,
    window_offset,
):
    bias_start_t = jnp.transpose(bias_start, (1, 2, 0))
    bias_end_t = jnp.transpose(bias_end, (1, 2, 0))
    rows_f32 = pltpu.VMEM((N * R, C), f32)
    bias_sum = pltpu.VMEM((H, N, N), f32)
    weight_sum = pltpu.VMEM((WEIGHT_BLOCKS, C, C), f32)
    bias_packed = pltpu.VMEM((N * CHUNKS, C), f32)
    weight_packed = pltpu.VMEM((PEERS * WEIGHT_ROWS, C), f32)
    term_rows = PEERS * CHUNKS

    send, penalty = call(
        start_forward_kernel,
        (struct((PEERS, 2 * R * R, C), bf16), struct((N, C), f32)),
        (pltpu.VMEM((2 * R, N, C), f32), rows_f32, rows_f32),
        {4: pltpu.SMEM},
    )(pair_act, cotangent, bias_start_t, residue_mask.reshape(CHAIN // C, C), window_offset, w_in_start, w_out_start)
    recv = exchange(send)
    grad_send, end_give, end_keep = call(
        end_kernel,
        (
            struct((PEERS, R * R, C), bf16),
            struct((BIAS_HALF + WEIGHT_HALF, C), bf16),
            struct((BIAS_HALF + WEIGHT_HALF, C), f32),
        ),
        (rows_f32, rows_f32, pltpu.VMEM((R, N, C), f32), rows_f32, bias_sum, weight_sum, bias_packed),
    )(recv, bias_end_t, penalty, w_in_end, w_in_end.T, w_out_end.T)
    grad_recv = exchange(grad_send)
    end_got = swap(end_give)
    grad_pair, term_send, start_give, start_keep = call(
        start_kernel,
        (
            struct((R, N, C), bf16),
            struct((PEERS, TERM_ROWS, C), bf16),
            struct((BIAS_HALF, C), bf16),
            struct((BIAS_HALF, C), f32),
        ),
        (rows_f32, bias_sum, weight_sum, bias_packed, weight_packed),
    )(pair_act, grad_recv, bias_start_t, penalty, w_in_start, w_in_start.T, w_out_start.T, end_keep, end_got)
    term_recv = exchange(term_send)
    start_got = swap(start_give)
    last_rows = R * CHUNKS + TOTAL_ROWS
    last_send, grad_bias_end = call(
        middle_kernel, (struct((CHIPS, last_rows, C), bf16), struct((R, H, N), f32))
    )(term_recv, start_keep, start_got)
    last_recv = exchange(last_send, "chip")
    totals = call(totals_kernel, struct((CHIPS, TOTAL_ROWS, C), bf16))(last_recv)
    totals = lax.all_gather(totals, "core", axis=0, tiled=True)
    grad_bias_start, *weights = call(
        last_kernel,
        (struct((R, H, N), f32),) + tuple(struct(shape, f32) for shape in ((C, 4 * C), (C, C), (C, 4 * C), (C, C))),
        (pltpu.VMEM((PEERS * TOTAL_ROWS, C), f32), pltpu.VMEM((C, C), f32)),
    )(last_recv, totals)
    return (grad_pair, grad_bias_start, grad_bias_end, *weights)


def solution(mesh):
    dp, dap = mesh.devices.shape
    fine = jax.sharding.Mesh(mesh.devices.reshape(dp, dap // 2, 2), ("dp", "chip", "core"))
    rows = P(("dp", "chip", "core"), None, None)
    placed = (rows, rows, P("dp", None, None), P("dp", None, None), P(), P(), P(), P(), P("dp"), P("dp"))
    return jax.shard_map(
        shards,
        mesh=fine,
        in_specs=placed,
        out_specs=(rows, rows, rows, P("dp", None), P("dp", None), P("dp", None), P("dp", None)),
        check_vma=False,
    )
```

```python
import functools

import jax
import jax.numpy as jnp
from jax import lax
from jax.experimental import pallas as pl
from jax.experimental.pallas import tpu as pltpu
from jax.sharding import PartitionSpec as P

H = 4
DH = 32
N = 256
C = 128
CHAIN = 4096
R = 4
PEERS = N // R

LN_EPSILON = 1e-05
MASK_PENALTY = 1000000000.0

f32 = jnp.float32
bf16 = jnp.bfloat16

VMEM_LIMIT = 20 * 1024 * 1024

GROUP = 4


def dot(a, b, dims):
    return lax.dot_general(a, b, (dims, ((), ())), preferred_element_type=f32)


def nn(a, b):
    return dot(a, b, ((1,), (0,)))


def nt(a, b):
    return dot(a, b, ((1,), (1,)))


def head_masks():
    lane = lax.broadcasted_iota(jnp.int32, (N, C), 1) // DH
    return [lane == h for h in range(H)]


def masked(value, masks):
    zero = jnp.zeros_like(value)
    return [jnp.where(m, value, zero) for m in masks]


def layer_stats(values):
    centred = values - jnp.mean(values, axis=-1, keepdims=True)
    inv_std = lax.rsqrt(jnp.mean(centred * centred, axis=-1, keepdims=True) + LN_EPSILON)
    return centred * inv_std, inv_std


def project(normed, w_in):
    projected = nn(normed, w_in)
    queries = (projected[:, :C] * DH ** (-0.5)).astype(bf16)
    keys = projected[:, C : 2 * C].astype(bf16)
    values = projected[:, 2 * C : 3 * C].astype(bf16)
    gate = 1.0 / (1.0 + jnp.exp(-projected[:, 3 * C :]))
    return queries, keys, values, gate


def pack_rows(value, r, stage, packed):
    stage[...] = value
    for residue in range(R):
        packed[pl.ds(r * R + residue, PEERS, stride=R * R), :] = stage[pl.ds(residue, PEERS, stride=R), :]


def softmax_all(keys_h, queries, bias_ref, penalty):
    scores = []
    for r in range(len(queries)):
        both = nt(jnp.concatenate(keys_h[r], axis=0), queries[r])
        scores.append([both[h * N : (h + 1) * N] for h in range(H)])
    return [[head_softmax(row[h], bias_ref[h], penalty) for h in range(H)] for row in scores]


def head_softmax(scores, bias_h, penalty):
    parts = []
    for first in range(0, N, 128):
        at = slice(first, first + 128)
        block = scores[:, at] + bias_h[:, at].astype(f32) + penalty[:, at]
        exponent = jnp.exp(block - jnp.max(block, axis=0, keepdims=True))
        parts.append(exponent * (1.0 / jnp.sum(exponent, axis=0, keepdims=True)))
    return jnp.concatenate(parts, axis=1)


def attend_all(values_t, probs_b):
    parts = [
        [nn(values_t[r][h * DH : (h + 1) * DH], probs_b[r][h]) for h in range(H)] for r in range(len(values_t))
    ]
    return [jnp.concatenate(row, axis=0).T for row in parts]


def window_penalty(mask_ref, offset_ref):
    rows = CHAIN // C
    offset = offset_ref[0]
    first, shift = offset // C, offset % C
    back = jnp.where(shift == 0, 0, C - shift)
    lane = lax.broadcasted_iota(jnp.int32, (8, C), 1)
    turned = []
    for i in range(N // C + 1):
        row = jnp.broadcast_to(mask_ref[pl.ds(jnp.minimum(first + i, rows - 1), 1), :], (8, C))
        turned.append(pltpu.roll(row, back, 1))
    columns = []
    for i in range(N // C):
        window = jnp.where(lane + shift < C, turned[i], turned[i + 1])
        penalty = (window.astype(f32) - 1.0) * MASK_PENALTY
        columns.append(jnp.broadcast_to(penalty[:1], (C, C)).T)
    return jnp.concatenate(columns, axis=0)


def wide_penalty(penalty):
    return jnp.concatenate([penalty] * (N // C), axis=1)


def start_forward_kernel(
    x_ref, cot_ref, bias_ref, mask_ref, offset_ref, w_in_ref, w_out_ref,
    send_ref, pen_ref, stage, first_packed, cot_packed,
):
    masks = head_masks()
    column = window_penalty(mask_ref, offset_ref)
    pen_ref[...] = column
    penalty = wide_penalty(column)
    x = x_ref[...].reshape(R * N, C).astype(f32)
    normed, _ = layer_stats(x)
    queries, keys, values, gate = project(normed.astype(bf16), w_in_ref[...])
    attended = []
    for first in range(0, R, GROUP):
        rows = [slice(r * N, (r + 1) * N) for r in range(first, first + GROUP)]
        keys_h = [masked(keys[at], masks) for at in rows]
        values_t = [values[at].astype(f32).T.astype(bf16) for at in rows]
        probs = softmax_all(keys_h, [queries[at] for at in rows], bias_ref, penalty)
        attended += attend_all(values_t, [[p.astype(bf16) for p in row] for row in probs])
    gated = (gate * jnp.concatenate(attended, axis=0)).astype(bf16)
    out = (x + nn(gated, w_out_ref[...])).astype(bf16).astype(f32)
    for r in range(R):
        pack_rows(out[r * N : (r + 1) * N], r, stage.at[r], first_packed)
        pack_rows(cot_ref[r].astype(f32), r, stage.at[R + r], cot_packed)
    send_ref[:, : R * R, :] = first_packed[...].reshape(PEERS, R * R, C).astype(bf16)
    send_ref[:, R * R :, :] = cot_packed[...].reshape(PEERS, R * R, C).astype(bf16)


def node_states(x, bias_ref, penalty, w_in_ref, masks):
    count = x.shape[0] // N
    normed, inv_std = layer_stats(x)
    queries, keys, values, gate = project(normed.astype(bf16), w_in_ref[...])
    rows = [slice(r * N, (r + 1) * N) for r in range(count)]
    keys_h = [masked(keys[at], masks) for at in rows]
    values_t = [values[at].astype(f32).T.astype(bf16) for at in rows]
    keys_t = [keys[at].astype(f32).T.astype(bf16) for at in rows]
    probs = softmax_all(keys_h, [queries[at] for at in rows], bias_ref, penalty)
    attended = attend_all(values_t, [[p.astype(bf16) for p in row] for row in probs])
    return [
        (normed[at], inv_std[at], queries[at], keys_t[r], values[at], gate[at], attended[r], probs[r])
        for r, at in enumerate(rows)
    ]


def node_backward(first, states, upstreams, w_in_t_ref, w_out_t_ref, masks, bias_sum, weight_sum):
    count = len(states)
    normed, inv_std, queries, keys_t, values, gate, attended, probs = zip(*states)
    values_h = [masked(v, masks) for v in values]
    up_b = [u.astype(bf16) for u in upstreams]
    grad_gated = [nn(u, w_out_t_ref[...]) for u in up_b]
    gated = [(gate[r] * attended[r]).astype(bf16) for r in range(count)]
    grad_gate = [grad_gated[r] * attended[r] * gate[r] * (1.0 - gate[r]) for r in range(count)]
    grad_mixed = [(grad_gated[r] * gate[r]).astype(bf16) for r in range(count)]
    grad_probs = []
    for r in range(count):
        both = nt(jnp.concatenate(values_h[r], axis=0), grad_mixed[r])
        grad_probs.append([both[h * N : (h + 1) * N] for h in range(H)])
    scores_b = [[None] * H for _ in range(count)]
    by_value = [[None] * H for _ in range(count)]
    by_key = [[None] * H for _ in range(count)]
    by_query = [[None] * H for _ in range(count)]
    for step in range(H + 2):
        if step < H:
            h, total = step, None
            for r in range(count):
                inner = jnp.sum(probs[r][h] * grad_probs[r][h], axis=0, keepdims=True)
                grad_scores = probs[r][h] * (grad_probs[r][h] - inner)
                scores_b[r][h] = grad_scores.astype(bf16)
                total = grad_scores if total is None else total + grad_scores
                by_value[r][h] = nn(probs[r][h].astype(bf16), grad_mixed[r])
            if first:
                bias_sum[h] = total
            else:
                bias_sum[h] += total
        if step >= 2:
            h = step - 2
            for r in range(count):
                by_key[r][h] = nn(scores_b[r][h], queries[r])
                by_query[r][h] = nn(keys_t[r][h * DH : (h + 1) * DH], scores_b[r][h])
    wins, wouts, grads = [], [], []
    for r in range(count):
        grad_value, grad_key = by_value[r][0], by_key[r][0]
        for h in range(1, H):
            grad_value = jnp.where(masks[h], by_value[r][h], grad_value)
            grad_key = jnp.where(masks[h], by_key[r][h], grad_key)
        grad_query = jnp.concatenate(by_query[r], axis=0).T * DH ** (-0.5)
        grad_proj = jnp.concatenate([grad_query, grad_key, grad_value, grad_gate[r]], axis=-1).astype(bf16)
        wins.append(nn(normed[r].T.astype(bf16), grad_proj))
        wouts.append(nn(gated[r].astype(f32).T.astype(bf16), up_b[r]))
        grad_normed = nn(grad_proj, w_in_t_ref[...])
        centred = (
            grad_normed
            - jnp.mean(grad_normed, axis=-1, keepdims=True)
            - normed[r] * jnp.mean(grad_normed * normed[r], axis=-1, keepdims=True)
        )
        grads.append(upstreams[r] + inv_std[r] * centred)
    win, wout = sum(wins[1:], wins[0]), sum(wouts[1:], wouts[0])
    blocks = [win[:, q * C : (q + 1) * C] for q in range(4)] + [wout]
    for q, block in enumerate(blocks):
        if first:
            weight_sum[q] = block
        else:
            weight_sum[q] += block
    return grads


CHUNKS = H * N // C
WEIGHT_BLOCKS = 5
BIAS_HALF = 2 * PEERS * CHUNKS
WEIGHT_HALF = WEIGHT_BLOCKS * PEERS
WEIGHT_ROWS = 16
TERM_ROWS = 2 * CHUNKS + WEIGHT_ROWS
TOTAL_ROWS = WEIGHT_ROWS + CHUNKS


CHIPS = PEERS // 2


def core_index():
    return lax.axis_index("core")


def bias_terms(bias_sum, bias_packed):
    eye = (lax.broadcasted_iota(jnp.int32, (N, N), 0) == lax.broadcasted_iota(jnp.int32, (N, N), 1)).astype(bf16)
    for h in range(H):
        by_query = nt(eye, bias_sum[h].astype(bf16))
        for half in range(N // C):
            bias_packed[pl.ds(half * H + h, N, stride=CHUNKS), :] = by_query[:, half * C : (half + 1) * C]
    return bias_packed[...].reshape(PEERS, R, CHUNKS, C)


def core_split(even, odd, core, keep_ref, give_ref, rows):
    keep_ref[rows, :] = jnp.where(core == 0, even, odd)
    give_ref[rows, :] = jnp.where(core == 0, odd, even).astype(bf16)


def end_kernel(
    recv_ref, bias_ref, pen_ref, w_in_ref, w_in_t_ref, w_out_t_ref,
    send_ref, give_ref, keep_ref,
    x_all, up_all, stage, grad_packed, bias_sum, weight_sum, bias_packed,
):
    masks = head_masks()
    core = core_index()
    penalty = wide_penalty(pen_ref[...])
    x_all[...] = recv_ref[:, : R * R, :].astype(f32).reshape(N * R, C)
    up_all[...] = recv_ref[:, R * R :, :].astype(f32).reshape(N * R, C)
    for first in range(0, R, GROUP):
        group = range(first, first + GROUP)
        x = jnp.concatenate([x_all[pl.ds(r, N, stride=R), :] for r in group], axis=0)
        states = node_states(x, bias_ref, penalty, w_in_ref, masks)
        upstreams = [up_all[pl.ds(r, N, stride=R), :] for r in group]
        grads = node_backward(first == 0, states, upstreams, w_in_t_ref, w_out_t_ref, masks, bias_sum, weight_sum)
        for r, grad in zip(group, grads):
            pack_rows(grad, r, stage.at[r], grad_packed)
    send_ref[...] = grad_packed[...].reshape(PEERS, R * R, C).astype(bf16)
    terms = bias_terms(bias_sum, bias_packed)
    for parity in range(2):
        even, odd = (terms[:, 2 * parity + i].reshape(PEERS * CHUNKS, C) for i in range(2))
        core_split(even, odd, core, keep_ref, give_ref, pl.ds(parity * PEERS * CHUNKS, PEERS * CHUNKS))
    for q in range(WEIGHT_BLOCKS):
        even, odd = (weight_sum.at[q][pl.ds(i, PEERS, stride=2), :] for i in range(2))
        core_split(even, odd, core, keep_ref, give_ref, pl.ds(BIAS_HALF + q * PEERS, PEERS))


def start_kernel(
    x_ref, recv_ref, bias_ref, pen_ref, w_in_ref, w_in_t_ref, w_out_t_ref, end_keep_ref, end_got_ref,
    grad_ref, send_ref, give_ref, keep_ref,
    up_all, bias_sum, weight_sum, bias_packed, weight_packed,
):
    masks = head_masks()
    core = core_index()
    penalty = wide_penalty(pen_ref[...])
    up_all[...] = recv_ref[...].astype(f32).reshape(N * R, C)
    for first in range(0, R, GROUP):
        group = range(first, first + GROUP)
        x = x_ref[first : first + GROUP].reshape(GROUP * N, C).astype(f32)
        states = node_states(x, bias_ref, penalty, w_in_ref, masks)
        upstreams = [up_all[pl.ds(r, N, stride=R), :] for r in group]
        grads = node_backward(first == 0, states, upstreams, w_in_t_ref, w_out_t_ref, masks, bias_sum, weight_sum)
        for r, grad in zip(group, grads):
            grad_ref[r] = grad.astype(bf16)
    end_terms = end_keep_ref[...] + end_got_ref[...].astype(f32)
    weight_packed[...] = jnp.zeros_like(weight_packed)
    for q in range(WEIGHT_BLOCKS):
        for parity in range(2):
            block = weight_sum.at[q][pl.ds(parity, PEERS, stride=2), :]
            weight_packed[pl.ds(q * 2 + parity, PEERS, stride=WEIGHT_ROWS), :] = block
        block = end_terms[BIAS_HALF + q * PEERS : BIAS_HALF + (q + 1) * PEERS]
        weight_packed[pl.ds(2 * WEIGHT_BLOCKS + q, PEERS, stride=WEIGHT_ROWS), :] = block
    end_bias = by_parity(end_terms[:BIAS_HALF])
    weights = weight_packed[...].reshape(PEERS, WEIGHT_ROWS, C)
    send_ref[...] = jnp.concatenate(end_bias + [weights], axis=1).astype(bf16)
    terms = bias_terms(bias_sum, bias_packed).reshape(CHIPS, 2, R * CHUNKS, C)
    even, odd = (terms[:, i].reshape(BIAS_HALF, C) for i in range(2))
    core_split(even, odd, core, keep_ref, give_ref, slice(None))


def by_parity(rows):
    return [
        rows[parity * PEERS * CHUNKS : (parity + 1) * PEERS * CHUNKS].reshape(PEERS, CHUNKS, C) for parity in range(2)
    ]


def write_bias(rows, residue, out_ref):
    for half in range(N // C):
        out_ref[residue, :, half * C : (half + 1) * C] = rows[half * H : (half + 1) * H]


def middle_kernel(recv_ref, keep_ref, got_ref, send_ref, bias_ref):
    by_core = jnp.sum(recv_ref[...].astype(f32).reshape(CHIPS, 2, TERM_ROWS, C), axis=0)
    for parity in range(2):
        for core in range(2):
            write_bias(by_core[core, parity * CHUNKS : (parity + 1) * CHUNKS], 2 * parity + core, bias_ref)
    even, odd = by_core[0, 2 * CHUNKS :], by_core[1, 2 * CHUNKS :]
    slot = lax.broadcasted_iota(jnp.int32, (WEIGHT_ROWS, C), 0)
    totals = jnp.concatenate([even + jnp.where(slot < 2 * WEIGHT_BLOCKS, odd, 0.0), odd[CHUNKS:]], axis=0)
    bias_rows = (keep_ref[...] + got_ref[...].astype(f32)).reshape(CHIPS, R * CHUNKS, C)
    everyone = jnp.broadcast_to(totals[None], (CHIPS, TOTAL_ROWS, C))
    send_ref[...] = jnp.concatenate([bias_rows, everyone], axis=1).astype(bf16)


def totals_kernel(recv_ref, totals_ref):
    totals_ref[...] = recv_ref[...].astype(f32)[:, R * CHUNKS :].astype(bf16)


def last_kernel(recv_ref, totals_ref, bias_ref, in_start, out_start, in_end, out_end, stage, block):
    bias = jnp.sum(recv_ref[...].astype(f32)[:, : R * CHUNKS], axis=0)
    for residue in range(R):
        write_bias(bias[residue * CHUNKS : (residue + 1) * CHUNKS], residue, bias_ref)
    stage[...] = totals_ref[...].astype(f32).reshape(PEERS * TOTAL_ROWS, C) * (1.0 / N)
    end_slots = (2 * WEIGHT_BLOCKS, WEIGHT_ROWS + 2 * WEIGHT_BLOCKS - CHUNKS)
    for part, (win, wout) in enumerate(((in_start, out_start), (in_end, out_end))):
        for q in range(WEIGHT_BLOCKS):
            for core in range(2):
                for parity in range(2):
                    row = q * 2 + parity if part == 0 else end_slots[parity] + q
                    value = stage[pl.ds(core * CHIPS * TOTAL_ROWS + row, CHIPS, stride=TOTAL_ROWS), :]
                    block[pl.ds(2 * core + parity, CHIPS, stride=4), :] = value
            if q < 4:
                win[:, q * C : (q + 1) * C] = block[...]
            else:
                wout[...] = block[...]


def call(kernel, outs, scratch=(), places=None):
    vmem = pl.BlockSpec(memory_space=pltpu.VMEM)
    places = places or {}

    def apply(*operands):
        return pl.pallas_call(
            kernel,
            out_shape=outs,
            in_specs=[pl.BlockSpec(memory_space=places[i]) if i in places else vmem for i in range(len(operands))],
            out_specs=jax.tree.map(lambda _: vmem, outs),
            scratch_shapes=list(scratch),
            compiler_params=pltpu.CompilerParams(vmem_limit_bytes=VMEM_LIMIT),
        )(*operands)

    return apply


def struct(shape, dtype):
    return jax.ShapeDtypeStruct(shape, dtype)


def exchange(value, axes=("chip", "core")):
    rows = value.reshape(-1, C)
    return lax.all_to_all(rows, axes, split_axis=0, concat_axis=0, tiled=True).reshape(value.shape)


def swap(value):
    return lax.ppermute(value, "core", [(0, 1), (1, 0)])


def shards(
    pair_act,
    cotangent,
    bias_start,
    bias_end,
    w_in_start,
    w_out_start,
    w_in_end,
    w_out_end,
    residue_mask,
    window_offset,
):
    bias_start_t = jnp.transpose(bias_start, (1, 2, 0))
    bias_end_t = jnp.transpose(bias_end, (1, 2, 0))
    rows_f32 = pltpu.VMEM((N * R, C), f32)
    bias_sum = pltpu.VMEM((H, N, N), f32)
    weight_sum = pltpu.VMEM((WEIGHT_BLOCKS, C, C), f32)
    bias_packed = pltpu.VMEM((N * CHUNKS, C), f32)
    weight_packed = pltpu.VMEM((PEERS * WEIGHT_ROWS, C), f32)
    term_rows = PEERS * CHUNKS

    send, penalty = call(
        start_forward_kernel,
        (struct((PEERS, 2 * R * R, C), bf16), struct((N, C), f32)),
        (pltpu.VMEM((2 * R, N, C), f32), rows_f32, rows_f32),
        {4: pltpu.SMEM},
    )(pair_act, cotangent, bias_start_t, residue_mask.reshape(CHAIN // C, C), window_offset, w_in_start, w_out_start)
    recv = exchange(send)
    grad_send, end_give, end_keep = call(
        end_kernel,
        (
            struct((PEERS, R * R, C), bf16),
            struct((BIAS_HALF + WEIGHT_HALF, C), bf16),
            struct((BIAS_HALF + WEIGHT_HALF, C), f32),
        ),
        (rows_f32, rows_f32, pltpu.VMEM((R, N, C), f32), rows_f32, bias_sum, weight_sum, bias_packed),
    )(recv, bias_end_t, penalty, w_in_end, w_in_end.T, w_out_end.T)
    grad_recv = exchange(grad_send)
    end_got = swap(end_give)
    grad_pair, term_send, start_give, start_keep = call(
        start_kernel,
        (
            struct((R, N, C), bf16),
            struct((PEERS, TERM_ROWS, C), bf16),
            struct((BIAS_HALF, C), bf16),
            struct((BIAS_HALF, C), f32),
        ),
        (rows_f32, bias_sum, weight_sum, bias_packed, weight_packed),
    )(pair_act, grad_recv, bias_start_t, penalty, w_in_start, w_in_start.T, w_out_start.T, end_keep, end_got)
    term_recv = exchange(term_send)
    start_got = swap(start_give)
    last_rows = R * CHUNKS + TOTAL_ROWS
    last_send, grad_bias_end = call(
        middle_kernel, (struct((CHIPS, last_rows, C), bf16), struct((R, H, N), f32))
    )(term_recv, start_keep, start_got)
    last_recv = exchange(last_send, "chip")
    totals = call(totals_kernel, struct((CHIPS, TOTAL_ROWS, C), bf16))(last_recv)
    totals = lax.all_gather(totals, "core", axis=0, tiled=True)
    grad_bias_start, *weights = call(
        last_kernel,
        (struct((R, H, N), f32),) + tuple(struct(shape, f32) for shape in ((C, 4 * C), (C, C), (C, 4 * C), (C, C))),
        (pltpu.VMEM((PEERS * TOTAL_ROWS, C), f32), pltpu.VMEM((C, C), f32)),
    )(last_recv, totals)
    return (grad_pair, grad_bias_start, grad_bias_end, *weights)


def solution(mesh):
    dp, dap = mesh.devices.shape
    fine = jax.sharding.Mesh(mesh.devices.reshape(dp, dap // 2, 2), ("dp", "chip", "core"))
    rows = P(("dp", "chip", "core"), None, None)
    placed = (rows, rows, P("dp", None, None), P("dp", None, None), P(), P(), P(), P(), P("dp"), P("dp"))
    return jax.shard_map(
        shards,
        mesh=fine,
        in_specs=placed,
        out_specs=(rows, rows, rows, P("dp", None), P("dp", None), P("dp", None), P("dp", None)),
        check_vma=False,
    )
```

```python
import functools

import jax
import jax.numpy as jnp
from jax import lax
from jax.experimental import pallas as pl
from jax.experimental.pallas import tpu as pltpu
from jax.sharding import PartitionSpec as P

H = 4
DH = 32
N = 256
C = 128
CHAIN = 4096
R = 4
PEERS = N // R

LN_EPSILON = 1e-05
MASK_PENALTY = 1000000000.0

f32 = jnp.float32
bf16 = jnp.bfloat16

VMEM_LIMIT = 20 * 1024 * 1024

GROUP = 4


def dot(a, b, dims):
    return lax.dot_general(a, b, (dims, ((), ())), preferred_element_type=f32)


def nn(a, b):
    return dot(a, b, ((1,), (0,)))


def nt(a, b):
    return dot(a, b, ((1,), (1,)))


def head_masks():
    lane = lax.broadcasted_iota(jnp.int32, (N, C), 1) // DH
    return [lane == h for h in range(H)]


def masked(value, masks):
    zero = jnp.zeros_like(value)
    return [jnp.where(m, value, zero) for m in masks]


def layer_stats(values):
    centred = values - jnp.mean(values, axis=-1, keepdims=True)
    inv_std = lax.rsqrt(jnp.mean(centred * centred, axis=-1, keepdims=True) + LN_EPSILON)
    return centred * inv_std, inv_std


def project(normed, w_in):
    projected = nn(normed, w_in)
    queries = (projected[:, :C] * DH ** (-0.5)).astype(bf16)
    keys = projected[:, C : 2 * C].astype(bf16)
    values = projected[:, 2 * C : 3 * C].astype(bf16)
    gate = 1.0 / (1.0 + jnp.exp(-projected[:, 3 * C :]))
    return queries, keys, values, gate


def pack_rows(value, r, stage, packed):
    stage[...] = value
    for residue in range(R):
        packed[pl.ds(r * R + residue, PEERS, stride=R * R), :] = stage[pl.ds(residue, PEERS, stride=R), :]


def softmax_all(keys_h, queries, bias_ref, penalty):
    scores = []
    for r in range(len(queries)):
        both = nt(jnp.concatenate(keys_h[r], axis=0), queries[r])
        scores.append([both[h * N : (h + 1) * N] for h in range(H)])
    return [[head_softmax(row[h], bias_ref[h], penalty) for h in range(H)] for row in scores]


def head_softmax(scores, bias_h, penalty):
    parts = []
    for first in range(0, N, 128):
        at = slice(first, first + 128)
        block = scores[:, at] + bias_h[:, at].astype(f32) + penalty[:, at]
        exponent = jnp.exp(block - jnp.max(block, axis=0, keepdims=True))
        parts.append(exponent * (1.0 / jnp.sum(exponent, axis=0, keepdims=True)))
    return jnp.concatenate(parts, axis=1)


def attend_all(values_t, probs_b):
    parts = [
        [nn(values_t[r][h * DH : (h + 1) * DH], probs_b[r][h]) for h in range(H)] for r in range(len(values_t))
    ]
    return [jnp.concatenate(row, axis=0).T for row in parts]


def window_penalty(mask_ref, offset_ref):
    rows = CHAIN // C
    offset = offset_ref[0]
    first, shift = offset // C, offset % C
    back = jnp.where(shift == 0, 0, C - shift)
    lane = lax.broadcasted_iota(jnp.int32, (8, C), 1)
    turned = []
    for i in range(N // C + 1):
        row = jnp.broadcast_to(mask_ref[pl.ds(jnp.minimum(first + i, rows - 1), 1), :], (8, C))
        turned.append(pltpu.roll(row, back, 1))
    columns = []
    for i in range(N // C):
        window = jnp.where(lane + shift < C, turned[i], turned[i + 1])
        penalty = (window.astype(f32) - 1.0) * MASK_PENALTY
        columns.append(jnp.broadcast_to(penalty[:1], (C, C)).T)
    return jnp.concatenate(columns, axis=0)


def wide_penalty(penalty):
    return jnp.concatenate([penalty] * (N // C), axis=1)


TILE = 8


def spread(rows, ref):
    for i in range(rows.shape[1] // TILE):
        ref[:, :, i * C : (i + 1) * C] = rows[:, i * TILE : (i + 1) * TILE].astype(bf16)


def collect(ref, first, last):
    blocks = [ref[:, :, i * C : (i + 1) * C].astype(f32) for i in range(first // TILE, last // TILE)]
    return jnp.concatenate(blocks, axis=1)


def lanes(peers, rows):
    return struct((peers, TILE, rows // TILE * C), bf16)


def start_forward_kernel(
    x_ref, cot_ref, bias_ref, mask_ref, offset_ref, w_in_ref, w_out_ref,
    send_ref, pen_ref, stage, first_packed, cot_packed,
):
    masks = head_masks()
    column = window_penalty(mask_ref, offset_ref)
    pen_ref[...] = column
    penalty = wide_penalty(column)
    x = x_ref[...].reshape(R * N, C).astype(f32)
    normed, _ = layer_stats(x)
    queries, keys, values, gate = project(normed.astype(bf16), w_in_ref[...])
    attended = []
    for first in range(0, R, GROUP):
        rows = [slice(r * N, (r + 1) * N) for r in range(first, first + GROUP)]
        keys_h = [masked(keys[at], masks) for at in rows]
        values_t = [values[at].astype(f32).T.astype(bf16) for at in rows]
        probs = softmax_all(keys_h, [queries[at] for at in rows], bias_ref, penalty)
        attended += attend_all(values_t, [[p.astype(bf16) for p in row] for row in probs])
    gated = (gate * jnp.concatenate(attended, axis=0)).astype(bf16)
    out = (x + nn(gated, w_out_ref[...])).astype(bf16).astype(f32)
    for r in range(R):
        pack_rows(out[r * N : (r + 1) * N], r, stage.at[r], first_packed)
        pack_rows(cot_ref[r].astype(f32), r, stage.at[R + r], cot_packed)
    both = [part[...].reshape(PEERS, R * R, C) for part in (first_packed, cot_packed)]
    spread(jnp.concatenate(both, axis=1), send_ref)


def node_states(x, bias_ref, penalty, w_in_ref, masks):
    count = x.shape[0] // N
    normed, inv_std = layer_stats(x)
    queries, keys, values, gate = project(normed.astype(bf16), w_in_ref[...])
    rows = [slice(r * N, (r + 1) * N) for r in range(count)]
    keys_h = [masked(keys[at], masks) for at in rows]
    values_t = [values[at].astype(f32).T.astype(bf16) for at in rows]
    keys_t = [keys[at].astype(f32).T.astype(bf16) for at in rows]
    probs = softmax_all(keys_h, [queries[at] for at in rows], bias_ref, penalty)
    attended = attend_all(values_t, [[p.astype(bf16) for p in row] for row in probs])
    return [
        (normed[at], inv_std[at], queries[at], keys_t[r], values[at], gate[at], attended[r], probs[r])
        for r, at in enumerate(rows)
    ]


def node_backward(first, states, upstreams, w_in_t_ref, w_out_t_ref, masks, bias_sum, weight_sum):
    count = len(states)
    normed, inv_std, queries, keys_t, values, gate, attended, probs = zip(*states)
    values_h = [masked(v, masks) for v in values]
    up_b = [u.astype(bf16) for u in upstreams]
    grad_gated = [nn(u, w_out_t_ref[...]) for u in up_b]
    gated = [(gate[r] * attended[r]).astype(bf16) for r in range(count)]
    grad_gate = [grad_gated[r] * attended[r] * gate[r] * (1.0 - gate[r]) for r in range(count)]
    grad_mixed = [(grad_gated[r] * gate[r]).astype(bf16) for r in range(count)]
    grad_probs = []
    for r in range(count):
        both = nt(jnp.concatenate(values_h[r], axis=0), grad_mixed[r])
        grad_probs.append([both[h * N : (h + 1) * N] for h in range(H)])
    scores_b = [[None] * H for _ in range(count)]
    by_value = [[None] * H for _ in range(count)]
    by_key = [[None] * H for _ in range(count)]
    by_query = [[None] * H for _ in range(count)]
    for step in range(H + 2):
        if step < H:
            h, total = step, None
            for r in range(count):
                inner = jnp.sum(probs[r][h] * grad_probs[r][h], axis=0, keepdims=True)
                grad_scores = probs[r][h] * (grad_probs[r][h] - inner)
                scores_b[r][h] = grad_scores.astype(bf16)
                total = grad_scores if total is None else total + grad_scores
                by_value[r][h] = nn(probs[r][h].astype(bf16), grad_mixed[r])
            if first:
                bias_sum[h] = total
            else:
                bias_sum[h] += total
        if step >= 2:
            h = step - 2
            for r in range(count):
                by_key[r][h] = nn(scores_b[r][h], queries[r])
                by_query[r][h] = nn(keys_t[r][h * DH : (h + 1) * DH], scores_b[r][h])
    wins, wouts, grads = [], [], []
    for r in range(count):
        grad_value, grad_key = by_value[r][0], by_key[r][0]
        for h in range(1, H):
            grad_value = jnp.where(masks[h], by_value[r][h], grad_value)
            grad_key = jnp.where(masks[h], by_key[r][h], grad_key)
        grad_query = jnp.concatenate(by_query[r], axis=0).T * DH ** (-0.5)
        grad_proj = jnp.concatenate([grad_query, grad_key, grad_value, grad_gate[r]], axis=-1).astype(bf16)
        wins.append(nn(normed[r].T.astype(bf16), grad_proj))
        wouts.append(nn(gated[r].astype(f32).T.astype(bf16), up_b[r]))
        grad_normed = nn(grad_proj, w_in_t_ref[...])
        centred = (
            grad_normed
            - jnp.mean(grad_normed, axis=-1, keepdims=True)
            - normed[r] * jnp.mean(grad_normed * normed[r], axis=-1, keepdims=True)
        )
        grads.append(upstreams[r] + inv_std[r] * centred)
    win, wout = sum(wins[1:], wins[0]), sum(wouts[1:], wouts[0])
    blocks = [win[:, q * C : (q + 1) * C] for q in range(4)] + [wout]
    for q, block in enumerate(blocks):
        if first:
            weight_sum[q] = block
        else:
            weight_sum[q] += block
    return grads


CHUNKS = H * N // C
WEIGHT_BLOCKS = 5
BIAS_HALF = 2 * PEERS * CHUNKS
WEIGHT_HALF = WEIGHT_BLOCKS * PEERS
WEIGHT_ROWS = 16
TERM_ROWS = 2 * CHUNKS + WEIGHT_ROWS
TOTAL_ROWS = WEIGHT_ROWS + CHUNKS


CHIPS = PEERS // 2


def core_index():
    return lax.axis_index("core")


def bias_terms(bias_sum, bias_packed):
    eye = (lax.broadcasted_iota(jnp.int32, (N, N), 0) == lax.broadcasted_iota(jnp.int32, (N, N), 1)).astype(bf16)
    for h in range(H):
        by_query = nt(eye, bias_sum[h].astype(bf16))
        for half in range(N // C):
            bias_packed[pl.ds(half * H + h, N, stride=CHUNKS), :] = by_query[:, half * C : (half + 1) * C]
    return bias_packed[...].reshape(PEERS, R, CHUNKS, C)


def core_split(even, odd, core, keep_ref, give_ref, rows):
    keep_ref[rows, :] = jnp.where(core == 0, even, odd)
    give_ref[rows, :] = jnp.where(core == 0, odd, even).astype(bf16)


def end_kernel(
    recv_ref, bias_ref, pen_ref, w_in_ref, w_in_t_ref, w_out_t_ref,
    send_ref, give_ref, keep_ref,
    x_all, up_all, stage, grad_packed, bias_sum, weight_sum, bias_packed,
):
    masks = head_masks()
    core = core_index()
    penalty = wide_penalty(pen_ref[...])
    x_all[...] = collect(recv_ref, 0, R * R).reshape(N * R, C)
    up_all[...] = collect(recv_ref, R * R, 2 * R * R).reshape(N * R, C)
    for first in range(0, R, GROUP):
        group = range(first, first + GROUP)
        x = jnp.concatenate([x_all[pl.ds(r, N, stride=R), :] for r in group], axis=0)
        states = node_states(x, bias_ref, penalty, w_in_ref, masks)
        upstreams = [up_all[pl.ds(r, N, stride=R), :] for r in group]
        grads = node_backward(first == 0, states, upstreams, w_in_t_ref, w_out_t_ref, masks, bias_sum, weight_sum)
        for r, grad in zip(group, grads):
            pack_rows(grad, r, stage.at[r], grad_packed)
    spread(grad_packed[...].reshape(PEERS, R * R, C), send_ref)
    terms = bias_terms(bias_sum, bias_packed)
    for parity in range(2):
        even, odd = (terms[:, 2 * parity + i].reshape(PEERS * CHUNKS, C) for i in range(2))
        core_split(even, odd, core, keep_ref, give_ref, pl.ds(parity * PEERS * CHUNKS, PEERS * CHUNKS))
    for q in range(WEIGHT_BLOCKS):
        even, odd = (weight_sum.at[q][pl.ds(i, PEERS, stride=2), :] for i in range(2))
        core_split(even, odd, core, keep_ref, give_ref, pl.ds(BIAS_HALF + q * PEERS, PEERS))


def start_kernel(
    x_ref, recv_ref, bias_ref, pen_ref, w_in_ref, w_in_t_ref, w_out_t_ref, end_keep_ref, end_got_ref,
    grad_ref, send_ref, give_ref, keep_ref,
    up_all, bias_sum, weight_sum, bias_packed, weight_packed,
):
    masks = head_masks()
    core = core_index()
    penalty = wide_penalty(pen_ref[...])
    up_all[...] = collect(recv_ref, 0, R * R).reshape(N * R, C)
    for first in range(0, R, GROUP):
        group = range(first, first + GROUP)
        x = x_ref[first : first + GROUP].reshape(GROUP * N, C).astype(f32)
        states = node_states(x, bias_ref, penalty, w_in_ref, masks)
        upstreams = [up_all[pl.ds(r, N, stride=R), :] for r in group]
        grads = node_backward(first == 0, states, upstreams, w_in_t_ref, w_out_t_ref, masks, bias_sum, weight_sum)
        for r, grad in zip(group, grads):
            grad_ref[r] = grad.astype(bf16)
    end_terms = end_keep_ref[...] + end_got_ref[...].astype(f32)
    weight_packed[...] = jnp.zeros_like(weight_packed)
    for q in range(WEIGHT_BLOCKS):
        for parity in range(2):
            block = weight_sum.at[q][pl.ds(parity, PEERS, stride=2), :]
            weight_packed[pl.ds(q * 2 + parity, PEERS, stride=WEIGHT_ROWS), :] = block
        block = end_terms[BIAS_HALF + q * PEERS : BIAS_HALF + (q + 1) * PEERS]
        weight_packed[pl.ds(2 * WEIGHT_BLOCKS + q, PEERS, stride=WEIGHT_ROWS), :] = block
    end_bias = by_parity(end_terms[:BIAS_HALF])
    weights = weight_packed[...].reshape(PEERS, WEIGHT_ROWS, C)
    spread(jnp.concatenate(end_bias + [weights], axis=1), send_ref)
    terms = bias_terms(bias_sum, bias_packed).reshape(CHIPS, 2, R * CHUNKS, C)
    even, odd = (terms[:, i].reshape(BIAS_HALF, C) for i in range(2))
    core_split(even, odd, core, keep_ref, give_ref, slice(None))


def by_parity(rows):
    return [
        rows[parity * PEERS * CHUNKS : (parity + 1) * PEERS * CHUNKS].reshape(PEERS, CHUNKS, C) for parity in range(2)
    ]


def write_bias(rows, residue, out_ref):
    for half in range(N // C):
        out_ref[residue, :, half * C : (half + 1) * C] = rows[half * H : (half + 1) * H]


def middle_kernel(recv_ref, keep_ref, got_ref, send_ref, bias_ref):
    by_core = jnp.sum(collect(recv_ref, 0, TERM_ROWS).reshape(CHIPS, 2, TERM_ROWS, C), axis=0)
    for parity in range(2):
        for core in range(2):
            write_bias(by_core[core, parity * CHUNKS : (parity + 1) * CHUNKS], 2 * parity + core, bias_ref)
    even, odd = by_core[0, 2 * CHUNKS :], by_core[1, 2 * CHUNKS :]
    slot = lax.broadcasted_iota(jnp.int32, (WEIGHT_ROWS, C), 0)
    totals = jnp.concatenate([even + jnp.where(slot < 2 * WEIGHT_BLOCKS, odd, 0.0), odd[CHUNKS:]], axis=0)
    bias_rows = (keep_ref[...] + got_ref[...].astype(f32)).reshape(CHIPS, R * CHUNKS, C)
    everyone = jnp.broadcast_to(totals[None], (CHIPS, TOTAL_ROWS, C))
    spread(jnp.concatenate([bias_rows, everyone], axis=1), send_ref)


def totals_kernel(recv_ref, totals_ref):
    totals_ref[...] = collect(recv_ref, R * CHUNKS, R * CHUNKS + TOTAL_ROWS).astype(bf16)


def last_kernel(recv_ref, totals_ref, bias_ref, in_start, out_start, in_end, out_end, stage, block):
    bias = jnp.sum(collect(recv_ref, 0, R * CHUNKS), axis=0)
    for residue in range(R):
        write_bias(bias[residue * CHUNKS : (residue + 1) * CHUNKS], residue, bias_ref)
    stage[...] = totals_ref[...].astype(f32).reshape(PEERS * TOTAL_ROWS, C) * (1.0 / N)
    end_slots = (2 * WEIGHT_BLOCKS, WEIGHT_ROWS + 2 * WEIGHT_BLOCKS - CHUNKS)
    for part, (win, wout) in enumerate(((in_start, out_start), (in_end, out_end))):
        for q in range(WEIGHT_BLOCKS):
            for core in range(2):
                for parity in range(2):
                    row = q * 2 + parity if part == 0 else end_slots[parity] + q
                    value = stage[pl.ds(core * CHIPS * TOTAL_ROWS + row, CHIPS, stride=TOTAL_ROWS), :]
                    block[pl.ds(2 * core + parity, CHIPS, stride=4), :] = value
            if q < 4:
                win[:, q * C : (q + 1) * C] = block[...]
            else:
                wout[...] = block[...]


def call(kernel, outs, scratch=(), places=None):
    vmem = pl.BlockSpec(memory_space=pltpu.VMEM)
    places = places or {}

    def apply(*operands):
        return pl.pallas_call(
            kernel,
            out_shape=outs,
            in_specs=[pl.BlockSpec(memory_space=places[i]) if i in places else vmem for i in range(len(operands))],
            out_specs=jax.tree.map(lambda _: vmem, outs),
            scratch_shapes=list(scratch),
            compiler_params=pltpu.CompilerParams(vmem_limit_bytes=VMEM_LIMIT),
        )(*operands)

    return apply


def struct(shape, dtype):
    return jax.ShapeDtypeStruct(shape, dtype)


def exchange(value, axes=("chip", "core")):
    return lax.all_to_all(value, axes, split_axis=0, concat_axis=0, tiled=True)


def swap(value):
    return lax.ppermute(value, "core", [(0, 1), (1, 0)])


def shards(
    pair_act,
    cotangent,
    bias_start,
    bias_end,
    w_in_start,
    w_out_start,
    w_in_end,
    w_out_end,
    residue_mask,
    window_offset,
):
    bias_start_t = jnp.transpose(bias_start, (1, 2, 0))
    bias_end_t = jnp.transpose(bias_end, (1, 2, 0))
    rows_f32 = pltpu.VMEM((N * R, C), f32)
    bias_sum = pltpu.VMEM((H, N, N), f32)
    weight_sum = pltpu.VMEM((WEIGHT_BLOCKS, C, C), f32)
    bias_packed = pltpu.VMEM((N * CHUNKS, C), f32)
    weight_packed = pltpu.VMEM((PEERS * WEIGHT_ROWS, C), f32)
    term_rows = PEERS * CHUNKS

    send, penalty = call(
        start_forward_kernel,
        (lanes(PEERS, 2 * R * R), struct((N, C), f32)),
        (pltpu.VMEM((2 * R, N, C), f32), rows_f32, rows_f32),
        {4: pltpu.SMEM},
    )(pair_act, cotangent, bias_start_t, residue_mask.reshape(CHAIN // C, C), window_offset, w_in_start, w_out_start)
    recv = exchange(send)
    grad_send, end_give, end_keep = call(
        end_kernel,
        (
            lanes(PEERS, R * R),
            struct((BIAS_HALF + WEIGHT_HALF, C), bf16),
            struct((BIAS_HALF + WEIGHT_HALF, C), f32),
        ),
        (rows_f32, rows_f32, pltpu.VMEM((R, N, C), f32), rows_f32, bias_sum, weight_sum, bias_packed),
    )(recv, bias_end_t, penalty, w_in_end, w_in_end.T, w_out_end.T)
    grad_recv = exchange(grad_send)
    end_got = swap(end_give)
    grad_pair, term_send, start_give, start_keep = call(
        start_kernel,
        (
            struct((R, N, C), bf16),
            lanes(PEERS, TERM_ROWS),
            struct((BIAS_HALF, C), bf16),
            struct((BIAS_HALF, C), f32),
        ),
        (rows_f32, bias_sum, weight_sum, bias_packed, weight_packed),
    )(pair_act, grad_recv, bias_start_t, penalty, w_in_start, w_in_start.T, w_out_start.T, end_keep, end_got)
    term_recv = exchange(term_send)
    start_got = swap(start_give)
    last_rows = R * CHUNKS + TOTAL_ROWS
    last_send, grad_bias_end = call(
        middle_kernel, (lanes(CHIPS, last_rows), struct((R, H, N), f32))
    )(term_recv, start_keep, start_got)
    last_recv = exchange(last_send, "chip")
    totals = call(totals_kernel, struct((CHIPS, TOTAL_ROWS, C), bf16))(last_recv)
    totals = lax.all_gather(totals, "core", axis=0, tiled=True)
    grad_bias_start, *weights = call(
        last_kernel,
        (struct((R, H, N), f32),) + tuple(struct(shape, f32) for shape in ((C, 4 * C), (C, C), (C, 4 * C), (C, C))),
        (pltpu.VMEM((PEERS * TOTAL_ROWS, C), f32), pltpu.VMEM((C, C), f32)),
    )(last_recv, totals)
    return (grad_pair, grad_bias_start, grad_bias_end, *weights)


def solution(mesh):
    dp, dap = mesh.devices.shape
    fine = jax.sharding.Mesh(mesh.devices.reshape(dp, dap // 2, 2), ("dp", "chip", "core"))
    rows = P(("dp", "chip", "core"), None, None)
    placed = (rows, rows, P("dp", None, None), P("dp", None, None), P(), P(), P(), P(), P("dp"), P("dp"))
    return jax.shard_map(
        shards,
        mesh=fine,
        in_specs=placed,
        out_specs=(rows, rows, rows, P("dp", None), P("dp", None), P("dp", None), P("dp", None)),
        check_vma=False,
    )
```
